512 devices in a mesh: lon: 32 (over z, y_lo), lat: 4 (over x), lev: 4 (over y_hi, core).
Axes of the slice: x: 4, y: 4 (y_hi: 2, y_lo: 2; y = y_hi * 2 + y_lo), z: 16, core: 2. Of those that a mesh axis runs over, the one named last changes fastest.
Arguments:
- adjoint_in: float32 [8, 16, 16, 8192], P(None, 'lev', 'lat', 'lon'), may hold values from -6 to 6
- courant_lon: float32 [16, 16, 8192], P('lev', 'lat', 'lon'), may hold values from 0.05 to 0.45
- courant_lat: float32 [16, 16, 8192], P('lev', 'lat', 'lon'), may hold values from 0.05 to 0.25
- horiz_diff: float32 [8], replicated, may hold values from 0.01 to 0.06
- vert_diff: float32 [16], replicated, may hold values from 0.01 to 0.1
- innovations: bfloat16 [8192, 8, 16, 128], P(('lon', 'lat'), None, 'lev'), may hold values from -6 to 6
- obs_operator: bfloat16 [8192, 128, 256], P(('lon', 'lat')), may hold values from -0.5 to 0.5
- owner_tile: int32 [8192, 1], P(('lon', 'lat')), may hold values from 0 to 31; in each aligned block of 64 rows (0 to 63, 64 to 127, ...) at most 4 rows name the same one
- block_row: int32 [8192], P(('lon', 'lat')), may hold values from 0 to 3
- obs_count: int32 [8192], P(('lon', 'lat')), may hold values from 1 to 128
Outputs:
- adjoint_out: float32 [8, 16, 16, 8192], P(None, 'lev', 'lat', 'lon')
The draws below stay inside these ranges and needn't reach their ends.
Inputs may be any that keep to these rules, and one draw needn't show every extreme that they name: `owner_tile`: among the 64 blocks of one device at most 4 name the same longitude tile; in some device exactly 4 do.
All inputs are finite; a program needn't handle non-finite values.
Results may differ from the reference program's by a relative error of at most 0.002.
The reference program's roundings to bfloat16 on the way (of `observed` and `products`) count: a program that leaves them out, or rounds other values in their place, can miss the bound.
Values may be sent and summed in bfloat16 or wider, within the bound.
A program may use at most 64 MiB of HBM per device.

```python
import math
import jax
import jax.numpy as jnp
import numpy as np
from jax import lax

F = 8
OBS = 128
CLON = 256
STEPS = 3
CLAT = 4
BLK_DEV = 64
LEVELS = 16
NLAT = 16
NLON = 8192
NBLK = 8192
CAP = 4
N_LON = 32
N_LAT = 4


def set_ends(entries, rng, low, largest):
    spot = [jax.random.randint(jax.random.fold_in(rng, axis), (), 0, length) for axis, length in enumerate(entries.shape)]
    widest = entries.shape.index(max(entries.shape))
    neighbour = spot[:widest] + [(spot[widest] + 1) % entries.shape[widest]] + spot[widest + 1:]
    return entries.at[tuple(spot)].set(low).at[tuple(neighbour)].set(largest)


def shard_levels(stream_key, extent, shards, least, largest):
    def one(position, parts):
        heights = jax.random.uniform(jax.random.fold_in(jax.random.fold_in(stream_key, 6), position), (parts,), jnp.float32, least / len(shards), largest / len(shards))
        return jnp.repeat(jnp.exp(heights), extent[position] // parts).reshape((-1,) + (1,) * (len(extent) - position - 1))

    loudness = one(*shards[0])
    for cut in shards[1:]:
        loudness = loudness * one(*cut)
    return loudness


def routed_block(stream_key, own, number, rows, count, top, reach, lean):
    order = jax.random.permutation(stream_key, count)
    heavy_load, common = portions_of(count, rows * top, reach, lean, True), portions_of(count, rows * top, reach, lean, False)
    places = jnp.arange(count)

    def named(lengths, offset_by):
        used = int((lengths > 0).sum())
        fixed = max(1, used // 4)
        passed = fixed + (places - fixed + offset_by * (used - fixed)) % max(1, count - fixed)
        return jnp.zeros((count,), jnp.int32).at[order[jnp.where(places < fixed, places, passed)]].set(jnp.asarray(lengths, jnp.int32))

    lengths = jnp.where(number % 4 == 0, named(heavy_load, number // 4), named(common, number - number // 4 - 1))
    mixed = jax.random.permutation(jax.random.fold_in(own, 3), count)
    donor, sink = mixed[0:count // 2 * 2:2], mixed[1:count // 2 * 2:2]
    margin = jnp.minimum(lengths[donor] - 1, reach - lengths[sink]) // 2
    margin = jnp.where((donor == order[0]) | (sink == order[0]) | (lengths[sink] == 0), 0, jnp.maximum(margin, 0))
    passed = jax.random.randint(jax.random.fold_in(own, 4), (count // 2,), 0, 1 << 20) % (margin + 1)
    lengths = lengths.at[donor].add(-passed).at[sink].add(passed)
    labels = jnp.searchsorted(jnp.cumsum(lengths), jnp.arange(rows * top), side="right").astype(jnp.int32)
    grid = labels.reshape(top, rows).T
    grid = grid[jax.random.permutation(jax.random.fold_in(own, 1), rows)]
    offset_by = jax.random.randint(jax.random.fold_in(own, 2), (rows, 1), 0, top)
    return jnp.take_along_axis(grid, (jnp.arange(top)[None, :] + offset_by) % top, axis=1)


def portions_of(number_of, total, bound, lean, full):
    portions = [(1 << 20) // math.isqrt(rank ** lean) + 1 for rank in range(1, number_of + 1)]
    largest = bound if full else min(bound, max(-(-total // number_of), total * portions[0] // sum(portions)))
    least = 1 if total - largest >= number_of - 1 else 0
    given, spare = [largest] + [least] * (number_of - 1), total - largest - least * (number_of - 1)
    while spare > 0:
        free = [i for i in range(1, number_of) if given[i] < largest] or [i for i in range(1, number_of) if given[i] < bound]
        pool, budget = sum([portions[i] for i in free]), spare
        for i in free:
            addition = min(bound - given[i], max(1, budget * portions[i] // pool), spare)
            given[i] = given[i] + addition
            spare = spare - addition
    return np.array(given)


def noise(key, shape, spread, limit, split=(), held_as=jnp.bfloat16):
    values = jax.random.normal(key, shape, jnp.float32) * spread
    if len(split) > 0:
        values = shard_levels(key, shape, split, -0.22, 0.18) * values
    return jnp.clip(values, min=-limit, max=limit).astype(held_as)


def setup_inputs(seed: int = 0) -> dict:
    arg_keys = jax.random.split(jax.random.key(seed), 11)
    adjoint_in = noise(arg_keys[0], (F, LEVELS, NLAT, NLON), 1.0, 6.0, ((1, 4), (2, 4), (3, 32)), jnp.float32)
    courant_lon = jnp.clip(jnp.exp(math.log(0.45) - 2.1972245 * jax.random.uniform(arg_keys[1], (LEVELS, NLAT, NLON), jnp.float32) ** shard_levels(arg_keys[1], (LEVELS, NLAT, NLON), ((0, 4), (1, 4), (2, 32)), -0.2, 0.2)), 0.05, 0.45)
    courant_lat = jnp.clip(jnp.exp(math.log(0.25) - 1.609438 * jax.random.uniform(arg_keys[2], (LEVELS, NLAT, NLON), jnp.float32) ** shard_levels(arg_keys[2], (LEVELS, NLAT, NLON), ((0, 4), (1, 4), (2, 32)), -0.2, 0.2)), 0.05, 0.25)
    horiz_diff = jnp.clip(jnp.exp(jax.random.uniform(arg_keys[3], (F,), jnp.float32, math.log(0.01), math.log(0.06))), 0.01, 0.06)
    vert_diff = jnp.clip(jnp.exp(jax.random.uniform(arg_keys[4], (LEVELS,), jnp.float32, math.log(0.01), math.log(0.1))), 0.01, 0.1)
    innovations = noise(arg_keys[5], (NBLK, F, LEVELS, OBS), 1.0, 6.0, ((0, 128), (2, 4)))
    obs_operator = noise(arg_keys[6], (NBLK, OBS, CLON), OBS ** -0.5, 0.5, ((0, 128),))
    owner_tile_keys = jax.random.split(jax.random.fold_in(arg_keys[7], 1), NBLK // BLK_DEV)
    owner_tile_turns = jax.random.permutation(jax.random.fold_in(arg_keys[7], 3), NBLK // BLK_DEV)
    owner_tile = jax.vmap(lambda own, number: routed_block(jax.random.fold_in(arg_keys[7], 2), own, number, BLK_DEV, N_LON, 1, CAP, 2))(owner_tile_keys, owner_tile_turns).reshape((NBLK, 1))
    block_row = set_ends(jax.random.randint(arg_keys[8], (NBLK,), 0, CLAT), jax.random.fold_in(arg_keys[8], 1), 0, CLAT - 1).astype(jnp.int32)
    obs_count = set_ends(jax.random.randint(arg_keys[9], (NBLK,), 1, OBS + 1), jax.random.fold_in(arg_keys[9], 1), 1, OBS).astype(jnp.int32)
    return dict(adjoint_in=adjoint_in, courant_lon=courant_lon, courant_lat=courant_lat, horiz_diff=horiz_diff, vert_diff=vert_diff, innovations=innovations, obs_operator=obs_operator, owner_tile=owner_tile, block_row=block_row, obs_count=obs_count)


def adjoint_step(adjoint, courant_lon, courant_lat, horiz_diff, coef_up, coef_down):
    east_flux = courant_lon[None] * adjoint
    north_flux = courant_lat[None] * adjoint
    east_side = jnp.roll(adjoint, -1, axis=3)
    west_side = jnp.roll(adjoint, 1, axis=3)
    east_moved = jnp.roll(east_flux, -1, axis=3)
    zero_row = jnp.zeros_like(adjoint[:, :, :1])
    north_side = jnp.concatenate([adjoint[:, :, 1:], zero_row], axis=2)
    south_side = jnp.concatenate([zero_row, adjoint[:, :, :-1]], axis=2)
    north_moved = jnp.concatenate([north_flux[:, :, 1:], zero_row], axis=2)
    zero_level = jnp.zeros_like(adjoint[:, :1])
    level_above = jnp.concatenate([adjoint[:, 1:], zero_level], axis=1)
    level_below = jnp.concatenate([zero_level, adjoint[:, :-1]], axis=1)
    diff_gain = horiz_diff[:, None, None, None]
    result = adjoint - east_flux - north_flux + east_moved + north_moved
    result = result + diff_gain * (east_side + west_side + north_side + south_side - 4.0 * adjoint)
    result = result + coef_up[None, :, None, None] * (level_above - adjoint)
    result = result + coef_down[None, :, None, None] * (level_below - adjoint)
    return result


def reference(adjoint_in, courant_lon, courant_lat, horiz_diff, vert_diff, innovations, obs_operator, owner_tile, block_row, obs_count):
    groups = NBLK // BLK_DEV
    level_ids = jnp.arange(LEVELS, dtype=jnp.int32)
    coef_up = jnp.where(level_ids < LEVELS - 1, vert_diff, jnp.zeros_like(vert_diff))
    coef_down = jnp.concatenate([jnp.zeros((1,), vert_diff.dtype), vert_diff[:-1]])
    adjoint = adjoint_in
    for sub_step in range(STEPS):
        adjoint = adjoint_step(adjoint, courant_lon, courant_lat, horiz_diff, coef_up, coef_down)

    group_innov = innovations.reshape(groups, BLK_DEV, F, LEVELS, OBS)
    group_ops = obs_operator.reshape(groups, BLK_DEV, OBS, CLON)
    group_tiles = owner_tile[:, 0].reshape(groups, BLK_DEV)
    group_rows = block_row.reshape(groups, BLK_DEV)
    group_counts = obs_count.reshape(groups, BLK_DEV)
    group_ids = jnp.arange(groups, dtype=jnp.int32)

    def add_group(column_sum, group_items):
        group_id, block_innov, block_ops, lon_tiles, lat_rows, counts_here = group_items
        observed = jnp.arange(OBS, dtype=jnp.int32)[None, :] < counts_here[:, None]
        masked = jnp.where(observed[:, None, None, :], block_innov, jnp.zeros_like(block_innov))
        products = jnp.einsum("bfko,boc->fkbc", masked.astype(jnp.float32), block_ops.astype(jnp.float32)).astype(jnp.bfloat16)
        products = lax.optimization_barrier(products).astype(jnp.float32)
        global_rows = ((group_id % N_LAT) * CLAT + lat_rows).astype(jnp.int32)
        column_sum = column_sum.at[:, :, global_rows, lon_tiles.astype(jnp.int32), :].add(products)
        return column_sum, None

    start_sum = jnp.zeros((F, LEVELS, NLAT, N_LON, CLON), jnp.float32)
    column_sum, unused = lax.scan(add_group, start_sum, (group_ids, group_innov, group_ops, group_tiles, group_rows, group_counts))
    obs_gradient = column_sum.reshape(F, LEVELS, NLAT, NLON)
    return adjoint + obs_gradient
```

```python
import functools

import jax
import jax.numpy as jnp
from jax import lax
from jax.experimental import pallas as pl
from jax.experimental.pallas import tpu as pltpu
from jax.sharding import PartitionSpec as P

STEPS = 3
CAP = 4
SPLIT = 80
TOP = 32000.0
MESH = pl.DeviceIdType.MESH
F32 = jnp.float32


def encode(x):
    rows = x.shape[0]
    peak = jnp.max(jnp.abs(x).reshape(rows // 8, 8, 256), axis=0)
    peak = jnp.maximum(peak[:, :128], peak[:, 128:])
    peak = jnp.maximum(jnp.max(peak, axis=0, keepdims=True), 1e-30)
    gain = TOP / peak
    gain = jnp.concatenate([gain, gain], axis=1)
    return jnp.round(x * gain).astype(jnp.int32).astype(jnp.int16), peak * (1.0 / TOP)


def decode(ints, scale):
    scale = jnp.concatenate([scale, scale], axis=1)
    return ints.astype(jnp.int32).astype(F32) * scale


def kernel(
    sizes,
    vd_s,
    hd_s,
    row_s,
    adj_ref,
    cu_ref,
    cv_ref,
    inn_ref,
    own_ref,
    op_hbm,
    out_ref,
    ops,
    op_sem,
    prod,
    code_v,
    code_s,
    code_sem,
    mine,
    other,
    ysend,
    yrecv,
    y_sems,
    asend,
    arecv,
    bsend,
    brecv,
    scale_send,
    scale_recv,
    ring_send_sem,
    ring_recv_sem,
    scale_send_sem,
    scale_recv_sem,
    fsend,
    frecv,
    fscale_send,
    fscale_recv,
    f_sems,
    fields,
    lev_lo,
    lev_hi,
    lat_lo,
    lat_hi,
    wind_send,
    wind_recv,
    lon_send,
    lon_recv,
    halo_send_sem,
    halo_recv_sem,
    wind_sems,
):
    n_lon, n_lat, n_lev = sizes
    nz = n_lon // 2
    half = nz // 2
    nb = prod.shape[0] - 1
    lon, lat, lev = (lax.axis_index(name) for name in ("lon", "lat", "lev"))
    z, yl = lon // 2, lon % 2
    partner = z * 2 + (1 - yl)
    ring = (((z + 1) % nz) * 2 + yl, ((z + nz - 1) % nz) * 2 + yl)
    east, west = (lon + 1) % n_lon, (lon + n_lon - 1) % n_lon

    groups = op_sem.shape[0]
    per = nb // groups

    def fetch(g):
        return pltpu.make_async_copy(
            op_hbm.at[pl.ds(g * per, per)], ops.at[pl.ds(g * per, per)], op_sem.at[g]
        )

    for g in range(groups):
        fetch(g).start()

    barrier = pltpu.get_barrier_semaphore()
    greet = [{"lon": t} for t in (ring[0], ring[1], east, west)]
    greet += [{"lat": (lat + 1) % n_lat}, {"lat": (lat + n_lat - 1) % n_lat}]
    greet += [{"lev": (lev + 1) % n_lev}, {"lev": (lev + n_lev - 1) % n_lev}]
    for target in greet:
        pl.semaphore_signal(barrier, inc=1, device_id=target, device_id_type=MESH)

    bi = lax.broadcasted_iota(jnp.int32, (nb, nb), 0)
    bj = lax.broadcasted_iota(jnp.int32, (nb, nb), 1)
    tcol = own_ref[...]
    trow = jnp.sum(jnp.where(bi == bj, tcol, 0), axis=0, keepdims=True)
    earlier = jnp.where((tcol == trow) & (bj < bi), 1.0, 0.0)
    place = jnp.sum(earlier, axis=1, keepdims=True).astype(jnp.int32)
    slot = lax.broadcasted_iota(jnp.int32, (nb, 128), 1)
    number = lax.broadcasted_iota(jnp.int32, (nb, 128), 0)
    hit = (tcol == slot // CAP) & (place == slot % CAP)
    code_v[...] = jnp.sum(jnp.where(hit, number - nb, 0), axis=0, keepdims=True) + nb
    to_smem = pltpu.make_async_copy(code_v, code_s, code_sem)
    to_smem.start()

    for j in range(4):
        for k in range(4):
            fields[0, j, k] = adj_ref[:, k, j, :]
    u_first = jnp.concatenate(
        [
            jnp.broadcast_to(cu_ref[k, pl.ds(j, 1), 0:128], (8, 128))
            for j in range(4)
            for k in range(4)
        ],
        axis=0,
    ).T[0:1]
    wind_send[...] = jnp.zeros_like(wind_send)
    for k in range(4):
        wind_send[pl.ds(k, 1)] = cv_ref[k, pl.ds(0, 1), :]
    at_south, at_north = lat == 0, lat == n_lat - 1
    at_low, at_high = lev == 0, lev == n_lev - 1

    @pl.when(at_south)
    def _():
        lat_lo[...] = jnp.zeros_like(lat_lo)

    @pl.when(at_north)
    def _():
        lat_hi[...] = jnp.zeros_like(lat_hi)
        wind_recv[...] = jnp.zeros_like(wind_recv)

    @pl.when(at_low)
    def _():
        lev_lo[...] = jnp.zeros_like(lev_lo)

    @pl.when(at_high)
    def _():
        lev_hi[...] = jnp.zeros_like(lev_hi)

    prod[nb] = jnp.zeros_like(prod[nb])

    def multiply(g, carry):
        fetch(g).wait()
        for i in range(per):
            b = g * per + i
            p = jnp.dot(inn_ref[b], ops[b], preferred_element_type=F32)
            prod[b] = p.astype(jnp.bfloat16).astype(F32)
        return carry

    lax.fori_loop(0, groups, multiply, 0)

    pl.semaphore_wait(barrier, len(greet))

    def halo(r):
        def copy(q, src, dst, target):
            return pltpu.make_async_remote_copy(
                src_ref=src,
                dst_ref=dst,
                send_sem=halo_send_sem.at[q, r],
                recv_sem=halo_recv_sem.at[q, r],
                device_id=target,
                device_id_type=MESH,
            )

        return (
            copy(0, fields.at[r, 3], lat_lo.at[r], {"lat": (lat + 1) % n_lat}),
            copy(1, fields.at[r, 0], lat_hi.at[r], {"lat": (lat + n_lat - 1) % n_lat}),
            copy(2, fields.at[r, :, 3], lev_lo.at[r], {"lev": (lev + 1) % n_lev}),
            copy(3, fields.at[r, :, 0], lev_hi.at[r], {"lev": (lev + n_lev - 1) % n_lev}),
            copy(4, lon_send.at[r, 0], lon_recv.at[r, 0], {"lon": east}),
            copy(5, lon_send.at[r, 1], lon_recv.at[r, 1], {"lon": west}),
        )

    wind = pltpu.make_async_remote_copy(
        src_ref=wind_send,
        dst_ref=wind_recv,
        send_sem=wind_sems.at[0],
        recv_sem=wind_sems.at[1],
        device_id={"lat": (lat + n_lat - 1) % n_lat},
        device_id_type=MESH,
    )
    sends = (~at_north, ~at_south, ~at_high, ~at_low, None, None)
    arrives = (~at_south, ~at_north, ~at_low, ~at_high, None, None)

    def gated(flag, action):
        if flag is None:
            action()
        else:
            pl.when(flag)(action)

    def send_halo(r):
        flat = fields[r].reshape(128, 256)
        first = flat[:, 0:128].T[0:1]
        last = flat[:, 128:256].T[127:128]
        lon_send[r, 0, pl.ds(0, 1)] = last
        lon_send[r, 1, pl.ds(0, 1)] = first
        lon_send[r, 1, pl.ds(1, 1)] = first * u_first
        for flag, copy in zip(sends, halo(r)):
            gated(flag, copy.start)

    lon_send[...] = jnp.zeros_like(lon_send)
    send_halo(0)
    gated(sends[1], wind.start)

    lane = lax.broadcasted_iota(jnp.int32, (8, 256), 1)
    field = lax.broadcasted_iota(jnp.int32, (8, 256), 0)
    gain = jnp.zeros((8, 256), F32)
    for f in range(8):
        gain = jnp.where(field == f, hd_s[f], gain)

    def sub_step(r):
        for flag, copy in zip(arrives, halo(r)):
            gated(flag, copy.wait_recv)
        edges = jnp.concatenate([lon_recv[r, 0], lon_recv[r, 1]], axis=0).T

        def at(j, k):
            if j < 0:
                return lat_lo[r, k]
            if j > 3:
                return lat_hi[r, k]
            if k < 0:
                return lev_lo[r, j]
            if k > 3:
                return lev_hi[r, j]
            return fields[r, j, k]

        def north_wind(j, k):
            return wind_recv[pl.ds(k, 1)] if j > 3 else cv_ref[k, pl.ds(j, 1), :]

        for k in range(4):
            level = lev * 4 + k
            up = jnp.where(level < n_lev * 4 - 1, vd_s[level], 0.0)
            down = jnp.where(level > 0, vd_s[jnp.maximum(level - 1, 0)], 0.0)
            for j in range(4):
                a = at(j, k)
                rows = slice((j * 4 + k) * 8, (j * 4 + k) * 8 + 8)
                flux = cu_ref[k, pl.ds(j, 1), :] * a
                north_flux = cv_ref[k, pl.ds(j, 1), :] * a
                north, south = at(j + 1, k), at(j - 1, k)
                a_east = jnp.where(lane == 255, edges[rows, 8:9], pltpu.roll(a, 255, 1))
                a_west = jnp.where(lane == 0, edges[rows, 0:1], pltpu.roll(a, 1, 1))
                moved = jnp.where(lane == 255, edges[rows, 9:10], pltpu.roll(flux, 255, 1))
                res = a - flux - north_flux + moved + north_wind(j + 1, k) * north
                res = res + gain * (a_east + a_west + north + south - 4.0 * a)
                res = res + up * (at(j, k + 1) - a)
                res = res + down * (at(j, k - 1) - a)
                fields[r + 1, j, k] = res

    def full_step(r):
        if isinstance(r, int):
            if r == 0:
                gated(arrives[1], wind.wait_recv)
        else:
            pl.when((r == 0) & ~at_north)(wind.wait_recv)
        sub_step(r)
        if isinstance(r, int):
            if r < STEPS - 1:
                send_halo(r + 1)
        else:
            pl.when(r < STEPS - 1)(lambda: send_halo(r + 1))

    to_smem.wait()

    def tile_sum(tile):
        total = [jnp.zeros((32, 256), F32) for j in range(4)]
        for c in range(CAP):
            b = code_s[0, tile * CAP + c]
            row = row_s[jnp.minimum(b, nb - 1)]
            p = prod[b]
            for j in range(4):
                total[j] = total[j] + p * jnp.where(row == j, 1.0, 0.0)
        return jnp.concatenate(total, axis=0)

    def ycopy(n):
        return pltpu.make_async_remote_copy(
            src_ref=ysend.at[n],
            dst_ref=yrecv.at[n],
            send_sem=y_sems.at[0, n],
            recv_sem=y_sems.at[1, n],
            device_id={"lon": partner},
            device_id_type=MESH,
        )

    def gather(n, carry):
        away = half - (n + 1) // 2
        dest = (z + nz + away * (2 * (n % 2) - 1)) % nz
        theirs = tile_sum(dest * 2 + (1 - yl))
        ysend[n] = theirs[:SPLIT].astype(jnp.bfloat16)
        ycopy(n).start()
        other[n] = theirs[SPLIT:]
        mine[n] = tile_sum(dest * 2 + yl)
        return carry

    def ring_copy(part, way, s):
        src, dst = ((asend, arecv), (bsend, brecv))[part]
        q = part * 2 + way
        data = pltpu.make_async_remote_copy(
            src_ref=src.at[way, s],
            dst_ref=dst.at[way, s],
            send_sem=ring_send_sem.at[q, s],
            recv_sem=ring_recv_sem.at[q, s],
            device_id={"lon": ring[way]},
            device_id_type=MESH,
        )
        scale = pltpu.make_async_remote_copy(
            src_ref=scale_send.at[q, s],
            dst_ref=scale_recv.at[q, s],
            send_sem=scale_send_sem.at[q, s],
            recv_sem=scale_recv_sem.at[q, s],
            device_id={"lon": ring[way]},
            device_id_type=MESH,
        )
        return data, scale

    def own_part(part, n):
        if part == 0:
            ycopy(n).wait_recv()
            return mine[n, :SPLIT] + yrecv[n].astype(F32)
        return jnp.concatenate([mine[n, SPLIT:], other[n]], axis=0)

    def arrived(part, way, s):
        for copy in ring_copy(part, way, s):
            copy.wait_recv()
        buf = (arecv, brecv)[part]
        return decode(buf[way, s], scale_recv[part * 2 + way, s])

    def ring_step(part, way, s, first):
        n = 2 * s - 1 + way
        if isinstance(s, int):
            n = max(n, 0)
        x = own_part(part, n)
        if not first:
            x = x + arrived(part, way, s - 1)
        ints, scale = encode(x)
        (asend, bsend)[part][way, s] = ints
        scale_send[part * 2 + way, s] = scale
        for copy in ring_copy(part, way, s):
            copy.start()

    def gather_range(lo, hi):
        lax.fori_loop(lo, hi, gather, 0)

    gather_range(0, min(5, nz))
    ring_step(1, 1, 0, True)
    ring_step(0, 0, 0, True)
    gather_range(min(5, nz), min(7, nz))
    ring_step(1, 1, 1, False)
    ring_step(1, 0, 1, True)
    ring_step(0, 0, 1, False)
    ring_step(0, 1, 1, True)
    gather_range(min(7, nz), min(9, nz))

    def later(s, carry):
        for part in (1, 0):
            for way in (0, 1):
                ring_step(part, way, s, False)
        lax.fori_loop(jnp.minimum(2 * s + 5, nz), jnp.minimum(2 * s + 7, nz), gather, 0)

        @pl.when((s % 2 == 0) & (s <= 2 * STEPS))
        def _():
            full_step(s // 2 - 1)

        return carry

    lax.fori_loop(2, half, later, 0)
    for r in range(sum(1 for s in range(2, half) if s % 2 == 0 and s <= 2 * STEPS), STEPS):
        full_step(r)

    last = half - 1
    line = own_part(1, nz - 1) + arrived(1, 0, last) + arrived(1, 1, last)
    rest = 128 - SPLIT
    ints, scale = encode(line[rest:])
    fsend[...] = ints
    fscale_send[...] = scale
    finals = [
        pltpu.make_async_remote_copy(
            src_ref=src,
            dst_ref=dst,
            send_sem=f_sems.at[q, 0],
            recv_sem=f_sems.at[q, 1],
            device_id={"lon": partner},
            device_id_type=MESH,
        )
        for q, (src, dst) in enumerate(((fsend, frecv), (fscale_send, fscale_recv)))
    ]
    for copy in finals:
        copy.start()
    result = fields[STEPS].reshape(128, 256)
    total = own_part(0, nz - 1) + arrived(0, 0, last) + arrived(0, 1, last)
    out_ref[:SPLIT] = result[:SPLIT] + total
    for copy in finals:
        copy.wait_recv()
    out_ref[SPLIT:] = result[SPLIT:] + line[:rest] + decode(frecv[...], fscale_recv[...])

    for copy in finals:
        copy.wait_send()

    def y_left(n, carry):
        ycopy(n).wait_send()
        return carry

    lax.fori_loop(0, nz, y_left, 0)

    def ring_left(s, carry):
        for part in range(2):
            for way in range(2):
                for copy in ring_copy(part, way, s):
                    copy.wait_send()
        return carry

    lax.fori_loop(1, half, ring_left, 0)
    for part in range(2):
        for copy in ring_copy(part, part, 0):
            copy.wait_send()
    gated(sends[1], wind.wait_send)

    def halo_left(r, carry):
        for flag, copy in zip(sends, halo(r)):
            gated(flag, copy.wait_send)
        return carry

    lax.fori_loop(0, STEPS, halo_left, 0)


def on_device(
    adjoint_in,
    courant_lon,
    courant_lat,
    horiz_diff,
    vert_diff,
    innovations,
    obs_operator,
    owner_tile,
    block_row,
    obs_count,
):
    nb, _, _, obs = innovations.shape
    sizes = tuple(lax.axis_size(name) for name in ("lon", "lat", "lev"))
    nz = sizes[0] // 2
    half = nz // 2
    rest = 128 - SPLIT
    observed = jnp.arange(obs, dtype=jnp.int32)[None, :] < obs_count[:, None]
    masked = jnp.where(observed[:, None, None, :], innovations, jnp.zeros((), jnp.bfloat16))
    masked = masked.transpose(0, 2, 1, 3).reshape(nb, 32, obs)

    vmem = pl.BlockSpec(memory_space=pltpu.VMEM)
    smem = pl.BlockSpec(memory_space=pltpu.SMEM)
    hbm = pl.BlockSpec(memory_space=pl.ANY)
    dma = pltpu.SemaphoreType.DMA
    i16, bf16, f32 = jnp.int16, jnp.bfloat16, jnp.float32
    out = pl.pallas_call(
        functools.partial(kernel, sizes),
        out_shape=jax.ShapeDtypeStruct((128, 256), f32),
        in_specs=[smem, smem, smem, vmem, vmem, vmem, vmem, vmem, hbm],
        out_specs=vmem,
        scratch_shapes=[
            pltpu.VMEM(obs_operator.shape, bf16),
            dma((8,)),
            pltpu.VMEM((nb + 1, 32, 256), f32),
            pltpu.VMEM((1, 128), jnp.int32),
            pltpu.SMEM((1, 128), jnp.int32),
            dma,
            pltpu.VMEM((nz, 128, 256), f32),
            pltpu.VMEM((nz, rest, 256), f32),
            pltpu.VMEM((nz, SPLIT, 256), bf16),
            pltpu.VMEM((nz, SPLIT, 256), bf16),
            dma((2, nz)),
            pltpu.VMEM((2, half, SPLIT, 256), i16),
            pltpu.VMEM((2, half, SPLIT, 256), i16),
            pltpu.VMEM((2, half, 2 * rest, 256), i16),
            pltpu.VMEM((2, half, 2 * rest, 256), i16),
            pltpu.VMEM((4, half, 1, 128), f32),
            pltpu.VMEM((4, half, 1, 128), f32),
            dma((4, half)),
            dma((4, half)),
            dma((4, half)),
            dma((4, half)),
            pltpu.VMEM((rest, 256), i16),
            pltpu.VMEM((rest, 256), i16),
            pltpu.VMEM((1, 128), f32),
            pltpu.VMEM((1, 128), f32),
            dma((2, 2)),
            pltpu.VMEM((STEPS + 1, 4, 4, 8, 256), f32),
            pltpu.VMEM((STEPS, 4, 8, 256), f32),
            pltpu.VMEM((STEPS, 4, 8, 256), f32),
            pltpu.VMEM((STEPS, 4, 8, 256), f32),
            pltpu.VMEM((STEPS, 4, 8, 256), f32),
            pltpu.VMEM((8, 256), f32),
            pltpu.VMEM((8, 256), f32),
            pltpu.VMEM((STEPS, 2, 8, 128), f32),
            pltpu.VMEM((STEPS, 2, 8, 128), f32),
            dma((6, STEPS)),
            dma((6, STEPS)),
            dma((2,)),
        ],
        compiler_params=pltpu.CompilerParams(
            collective_id=0, has_side_effects=True, vmem_limit_bytes=48 * 2**20
        ),
        name="adjoint",
    )(
        vert_diff,
        horiz_diff,
        block_row,
        adjoint_in,
        courant_lon,
        courant_lat,
        masked,
        owner_tile,
        obs_operator,
    )
    return out.reshape(4, 4, 8, 256).transpose(2, 1, 0, 3)


def solution(mesh):
    in_specs = (
        P(None, "lev", "lat", "lon"),
        P("lev", "lat", "lon"),
        P("lev", "lat", "lon"),
        P(),
        P(),
        P(("lon", "lat"), None, "lev", None),
        P(("lon", "lat"), None, None),
        P(("lon", "lat"), None),
        P(("lon", "lat")),
        P(("lon", "lat")),
    )
    out_specs = P(None, "lev", "lat", "lon")
    return jax.shard_map(
        on_device, mesh=mesh, in_specs=in_specs, out_specs=out_specs, check_vma=False
    )
```

```python
import functools

import jax
import jax.numpy as jnp
from jax import lax
from jax.experimental import pallas as pl
from jax.experimental.pallas import tpu as pltpu
from jax.sharding import PartitionSpec as P

STEPS = 3
CAP = 4
SPLIT = 80
TOP = 32000.0
MESH = pl.DeviceIdType.MESH
F32 = jnp.float32


def encode(x):
    rows = x.shape[0]
    peak = jnp.max(jnp.abs(x).reshape(rows // 8, 8, 256), axis=0)
    peak = jnp.maximum(peak[:, :128], peak[:, 128:])
    peak = jnp.maximum(jnp.max(peak, axis=0, keepdims=True), 1e-30)
    gain = TOP / peak
    gain = jnp.concatenate([gain, gain], axis=1)
    return jnp.round(x * gain).astype(jnp.int32).astype(jnp.int16), peak * (1.0 / TOP)


def decode(ints, scale):
    scale = jnp.concatenate([scale, scale], axis=1)
    return ints.astype(jnp.int32).astype(F32) * scale


def kernel(
    sizes,
    vd_s,
    hd_s,
    row_s,
    count_s,
    own_ref,
    adj_hbm,
    cu_hbm,
    cv_hbm,
    inn_hbm,
    op_hbm,
    out_ref,
    adj_ref,
    cu_ref,
    cv_ref,
    inn_ref,
    ops,
    in_sems,
    inn_sem,
    op_sem,
    prod,
    code_v,
    code_s,
    code_sem,
    mine,
    other,
    ysend,
    yrecv,
    y_sems,
    asend,
    arecv,
    bsend,
    brecv,
    scale_send,
    scale_recv,
    ring_send_sem,
    ring_recv_sem,
    scale_send_sem,
    scale_recv_sem,
    fsend,
    frecv,
    fscale_send,
    fscale_recv,
    f_sems,
    fields,
    lev_lo,
    lev_hi,
    lat_lo,
    lat_hi,
    wind_send,
    wind_recv,
    lon_send,
    lon_recv,
    halo_send_sem,
    halo_recv_sem,
    wind_sems,
    total_lo,
    total_hi,
):
    n_lon, n_lat, n_lev = sizes
    nz = n_lon // 2
    half = nz // 2
    nb = prod.shape[0] - 1
    lon, lat, lev = (lax.axis_index(name) for name in ("lon", "lat", "lev"))
    z, yl = lon // 2, lon % 2
    partner = z * 2 + (1 - yl)
    ring = (((z + 1) % nz) * 2 + yl, ((z + nz - 1) % nz) * 2 + yl)
    east, west = (lon + 1) % n_lon, (lon + n_lon - 1) % n_lon

    groups = op_sem.shape[0]
    per = nb // groups

    def fetch(g):
        part = pl.ds(g * per, per)
        return (
            pltpu.make_async_copy(inn_hbm.at[part], inn_ref.at[part], inn_sem.at[g]),
            pltpu.make_async_copy(op_hbm.at[part], ops.at[part], op_sem.at[g]),
        )

    state = [
        pltpu.make_async_copy(src, dst, in_sems.at[q])
        for q, (src, dst) in enumerate(((adj_hbm, adj_ref), (cu_hbm, cu_ref), (cv_hbm, cv_ref)))
    ]
    for g in range(groups):
        for copy in fetch(g):
            copy.start()
    for copy in state:
        copy.start()

    barrier = pltpu.get_barrier_semaphore()
    greet = [{"lon": t} for t in (ring[0], ring[1], east, west)]
    greet += [{"lat": (lat + 1) % n_lat}, {"lat": (lat + n_lat - 1) % n_lat}]
    greet += [{"lev": (lev + 1) % n_lev}, {"lev": (lev + n_lev - 1) % n_lev}]
    for target in greet:
        pl.semaphore_signal(barrier, inc=1, device_id=target, device_id_type=MESH)

    bi = lax.broadcasted_iota(jnp.int32, (nb, nb), 0)
    bj = lax.broadcasted_iota(jnp.int32, (nb, nb), 1)
    trow = own_ref[...]
    tcol = jnp.sum(jnp.where(bi == bj, trow, 0).astype(F32), axis=1, keepdims=True)
    tcol = tcol.astype(jnp.int32)
    earlier = jnp.where((tcol == trow) & (bj < bi), 1.0, 0.0)
    place = jnp.sum(earlier, axis=1, keepdims=True).astype(jnp.int32)
    slot = lax.broadcasted_iota(jnp.int32, (nb, 128), 1)
    number = lax.broadcasted_iota(jnp.int32, (nb, 128), 0)
    hit = (tcol == slot // CAP) & (place == slot % CAP)
    code_v[...] = jnp.sum(jnp.where(hit, number - nb, 0), axis=0, keepdims=True) + nb
    to_smem = pltpu.make_async_copy(code_v, code_s, code_sem)
    to_smem.start()

    prod[nb] = jnp.zeros_like(prod[nb])
    obs = ops.shape[1]
    observation = lax.broadcasted_iota(jnp.int32, (32, obs), 1)

    def multiply(g, carry):
        for copy in fetch(g):
            copy.wait()
        for i in range(per):
            b = g * per + i
            seen = inn_ref[b].astype(F32).reshape(32, obs)
            seen = jnp.where(observation < count_s[b], seen, 0.0).astype(jnp.bfloat16)
            p = jnp.dot(seen, ops[b], preferred_element_type=F32)
            prod[b] = p.astype(jnp.bfloat16).astype(F32)
        return carry

    lax.fori_loop(0, groups, multiply, 0)

    for copy in state:
        copy.wait()
    for j in range(4):
        for k in range(4):
            fields[0, j, k] = adj_ref[:, k, j, :]
    u_first = jnp.concatenate(
        [
            jnp.broadcast_to(cu_ref[k, pl.ds(j, 1), 0:128], (8, 128))
            for j in range(4)
            for k in range(4)
        ],
        axis=0,
    ).T[0:1]
    wind_send[...] = jnp.zeros_like(wind_send)
    for k in range(4):
        wind_send[pl.ds(k, 1)] = cv_ref[k, pl.ds(0, 1), :]
    at_south, at_north = lat == 0, lat == n_lat - 1
    at_low, at_high = lev == 0, lev == n_lev - 1

    @pl.when(at_south)
    def _():
        lat_lo[...] = jnp.zeros_like(lat_lo)

    @pl.when(at_north)
    def _():
        lat_hi[...] = jnp.zeros_like(lat_hi)
        wind_recv[...] = jnp.zeros_like(wind_recv)

    @pl.when(at_low)
    def _():
        lev_lo[...] = jnp.zeros_like(lev_lo)

    @pl.when(at_high)
    def _():
        lev_hi[...] = jnp.zeros_like(lev_hi)

    pl.semaphore_wait(barrier, len(greet))

    def halo(r):
        def copy(q, src, dst, target):
            return pltpu.make_async_remote_copy(
                src_ref=src,
                dst_ref=dst,
                send_sem=halo_send_sem.at[q, r],
                recv_sem=halo_recv_sem.at[q, r],
                device_id=target,
                device_id_type=MESH,
            )

        return (
            copy(0, fields.at[r, 3], lat_lo.at[r], {"lat": (lat + 1) % n_lat}),
            copy(1, fields.at[r, 0], lat_hi.at[r], {"lat": (lat + n_lat - 1) % n_lat}),
            copy(2, fields.at[r, :, 3], lev_lo.at[r], {"lev": (lev + 1) % n_lev}),
            copy(3, fields.at[r, :, 0], lev_hi.at[r], {"lev": (lev + n_lev - 1) % n_lev}),
            copy(4, lon_send.at[r, 0], lon_recv.at[r, 0], {"lon": east}),
            copy(5, lon_send.at[r, 1], lon_recv.at[r, 1], {"lon": west}),
        )

    wind = pltpu.make_async_remote_copy(
        src_ref=wind_send,
        dst_ref=wind_recv,
        send_sem=wind_sems.at[0],
        recv_sem=wind_sems.at[1],
        device_id={"lat": (lat + n_lat - 1) % n_lat},
        device_id_type=MESH,
    )
    sends = (~at_north, ~at_south, ~at_high, ~at_low, None, None)
    arrives = (~at_south, ~at_north, ~at_low, ~at_high, None, None)

    def gated(flag, action):
        if flag is None:
            action()
        else:
            pl.when(flag)(action)

    def send_halo(r):
        flat = fields[r].reshape(128, 256)
        first = flat[:, 0:128].T[0:1]
        last = flat[:, 128:256].T[127:128]
        lon_send[r, 0, pl.ds(0, 1)] = last
        lon_send[r, 1, pl.ds(0, 1)] = first
        lon_send[r, 1, pl.ds(1, 1)] = first * u_first
        for flag, copy in zip(sends, halo(r)):
            gated(flag, copy.start)

    lon_send[...] = jnp.zeros_like(lon_send)
    send_halo(0)
    gated(sends[1], wind.start)

    lane = lax.broadcasted_iota(jnp.int32, (8, 256), 1)
    field = lax.broadcasted_iota(jnp.int32, (8, 256), 0)
    gain = jnp.zeros((8, 256), F32)
    for f in range(8):
        gain = jnp.where(field == f, hd_s[f], gain)

    def sub_step(r):
        for flag, copy in zip(arrives, halo(r)):
            gated(flag, copy.wait_recv)
        edges = jnp.concatenate([lon_recv[r, 0], lon_recv[r, 1]], axis=0).T

        def at(j, k):
            if j < 0:
                return lat_lo[r, k]
            if j > 3:
                return lat_hi[r, k]
            if k < 0:
                return lev_lo[r, j]
            if k > 3:
                return lev_hi[r, j]
            return fields[r, j, k]

        def north_wind(j, k):
            return wind_recv[pl.ds(k, 1)] if j > 3 else cv_ref[k, pl.ds(j, 1), :]

        for k in range(4):
            level = lev * 4 + k
            up = jnp.where(level < n_lev * 4 - 1, vd_s[level], 0.0)
            down = jnp.where(level > 0, vd_s[jnp.maximum(level - 1, 0)], 0.0)
            for j in range(4):
                a = at(j, k)
                rows = slice((j * 4 + k) * 8, (j * 4 + k) * 8 + 8)
                flux = cu_ref[k, pl.ds(j, 1), :] * a
                north_flux = cv_ref[k, pl.ds(j, 1), :] * a
                north, south = at(j + 1, k), at(j - 1, k)
                a_east = jnp.where(lane == 255, edges[rows, 8:9], pltpu.roll(a, 255, 1))
                a_west = jnp.where(lane == 0, edges[rows, 0:1], pltpu.roll(a, 1, 1))
                moved = jnp.where(lane == 255, edges[rows, 9:10], pltpu.roll(flux, 255, 1))
                res = a - flux - north_flux + moved + north_wind(j + 1, k) * north
                res = res + gain * (a_east + a_west + north + south - 4.0 * a)
                res = res + up * (at(j, k + 1) - a)
                res = res + down * (at(j, k - 1) - a)
                fields[r + 1, j, k] = res

    def full_step(r):
        if isinstance(r, int):
            if r == 0:
                gated(arrives[1], wind.wait_recv)
        else:
            pl.when((r == 0) & ~at_north)(wind.wait_recv)
        sub_step(r)
        if isinstance(r, int):
            if r < STEPS - 1:
                send_halo(r + 1)
        else:
            pl.when(r < STEPS - 1)(lambda: send_halo(r + 1))

    to_smem.wait()

    def tile_sum(tile):
        rows = [jnp.zeros((32, 256), F32) for j in range(4)]
        for c in range(CAP):
            b = code_s[0, tile * CAP + c]
            row = row_s[jnp.minimum(b, nb - 1)]
            p = prod[b]
            for j in range(4):
                rows[j] = rows[j] + p * jnp.where(row == j, 1.0, 0.0)
        return jnp.concatenate(rows, axis=0)

    def ycopy(n):
        return pltpu.make_async_remote_copy(
            src_ref=ysend.at[n],
            dst_ref=yrecv.at[n],
            send_sem=y_sems.at[0, n],
            recv_sem=y_sems.at[1, n],
            device_id={"lon": partner},
            device_id_type=MESH,
        )

    def gather(n, carry):
        away = half - (n + 1) // 2
        dest = (z + nz + away * (2 * (n % 2) - 1)) % nz
        theirs = tile_sum(dest * 2 + (1 - yl))
        ysend[n] = theirs[:SPLIT].astype(jnp.bfloat16)
        ycopy(n).start()
        other[n] = theirs[SPLIT:]
        mine[n] = tile_sum(dest * 2 + yl)
        return carry

    def ring_copy(part, way, s):
        src, dst = ((asend, arecv), (bsend, brecv))[part]
        q = part * 2 + way
        data = pltpu.make_async_remote_copy(
            src_ref=src.at[way, s],
            dst_ref=dst.at[way, s],
            send_sem=ring_send_sem.at[q, s],
            recv_sem=ring_recv_sem.at[q, s],
            device_id={"lon": ring[way]},
            device_id_type=MESH,
        )
        scale = pltpu.make_async_remote_copy(
            src_ref=scale_send.at[q, s],
            dst_ref=scale_recv.at[q, s],
            send_sem=scale_send_sem.at[q, s],
            recv_sem=scale_recv_sem.at[q, s],
            device_id={"lon": ring[way]},
            device_id_type=MESH,
        )
        return data, scale

    def own_part(part, n):
        if part == 0:
            ycopy(n).wait_recv()
            return mine[n, :SPLIT] + yrecv[n].astype(F32)
        return jnp.concatenate([mine[n, SPLIT:], other[n]], axis=0)

    def arrived(part, way, s):
        for copy in ring_copy(part, way, s):
            copy.wait_recv()
        buf = (arecv, brecv)[part]
        return decode(buf[way, s], scale_recv[part * 2 + way, s])

    def ring_step(part, way, s, first):
        n = 2 * s - 1 + way
        if isinstance(s, int):
            n = max(n, 0)
        x = own_part(part, n)
        if not first:
            x = x + arrived(part, way, s - 1)
        ints, scale = encode(x)
        (asend, bsend)[part][way, s] = ints
        scale_send[part * 2 + way, s] = scale
        for copy in ring_copy(part, way, s):
            copy.start()

    def gather_range(lo, hi):
        lax.fori_loop(lo, hi, gather, 0)

    gather_range(0, min(5, nz))
    ring_step(1, 1, 0, True)
    ring_step(0, 0, 0, True)
    gather_range(min(5, nz), min(7, nz))
    ring_step(1, 1, 1, False)
    ring_step(1, 0, 1, True)
    ring_step(0, 0, 1, False)
    ring_step(0, 1, 1, True)
    gather_range(min(7, nz), min(9, nz))

    def later(s, carry):
        for part in (1, 0):
            for way in (0, 1):
                ring_step(part, way, s, False)
        lax.fori_loop(jnp.minimum(2 * s + 5, nz), jnp.minimum(2 * s + 7, nz), gather, 0)

        @pl.when((s % 2 == 0) & (s <= 2 * STEPS))
        def _():
            full_step(s // 2 - 1)

        return carry

    lax.fori_loop(2, half, later, 0)
    for r in range(sum(1 for s in range(2, half) if s % 2 == 0 and s <= 2 * STEPS), STEPS):
        full_step(r)

    last = half - 1
    line = own_part(1, nz - 1) + arrived(1, 0, last) + arrived(1, 1, last)
    rest = 128 - SPLIT
    ints, scale = encode(line[rest:])
    fsend[...] = ints
    fscale_send[...] = scale
    finals = [
        pltpu.make_async_remote_copy(
            src_ref=src,
            dst_ref=dst,
            send_sem=f_sems.at[q, 0],
            recv_sem=f_sems.at[q, 1],
            device_id={"lon": partner},
            device_id_type=MESH,
        )
        for q, (src, dst) in enumerate(((fsend, frecv), (fscale_send, fscale_recv)))
    ]
    for copy in finals:
        copy.start()
    direct = own_part(0, nz - 1) + arrived(0, 0, last) + arrived(0, 1, last)
    total_lo[:SPLIT], total_hi[:SPLIT] = direct[:, :128], direct[:, 128:]
    for copy in finals:
        copy.wait_recv()
    crossed = line[:rest] + decode(frecv[...], fscale_recv[...])
    total_lo[SPLIT:], total_hi[SPLIT:] = crossed[:, :128], crossed[:, 128:]
    for j in range(4):
        for k in range(4):
            pick = pl.ds(j * 32 + k, 8, stride=4)
            here = jnp.concatenate([total_lo[pick, :], total_hi[pick, :]], axis=1)
            out_ref[pl.ds((j * 4 + k) * 8, 8)] = fields[STEPS, j, k] + here

    for copy in finals:
        copy.wait_send()

    def y_left(n, carry):
        ycopy(n).wait_send()
        return carry

    lax.fori_loop(0, nz, y_left, 0)

    def ring_left(s, carry):
        for part in range(2):
            for way in range(2):
                for copy in ring_copy(part, way, s):
                    copy.wait_send()
        return carry

    lax.fori_loop(1, half, ring_left, 0)
    for part in range(2):
        for copy in ring_copy(part, part, 0):
            copy.wait_send()
    gated(sends[1], wind.wait_send)

    def halo_left(r, carry):
        for flag, copy in zip(sends, halo(r)):
            gated(flag, copy.wait_send)
        return carry

    lax.fori_loop(0, STEPS, halo_left, 0)


def on_device(
    adjoint_in,
    courant_lon,
    courant_lat,
    horiz_diff,
    vert_diff,
    innovations,
    obs_operator,
    owner_tile,
    block_row,
    obs_count,
):
    nb = innovations.shape[0]
    sizes = tuple(lax.axis_size(name) for name in ("lon", "lat", "lev"))
    nz = sizes[0] // 2
    half = nz // 2
    rest = 128 - SPLIT

    vmem = pl.BlockSpec(memory_space=pltpu.VMEM)
    smem = pl.BlockSpec(memory_space=pltpu.SMEM)
    hbm = pl.BlockSpec(memory_space=pltpu.HBM)
    dma = pltpu.SemaphoreType.DMA
    i16, bf16, f32 = jnp.int16, jnp.bfloat16, jnp.float32
    out = pl.pallas_call(
        functools.partial(kernel, sizes),
        out_shape=jax.ShapeDtypeStruct((128, 256), f32),
        in_specs=[smem, smem, smem, smem, vmem, hbm, hbm, hbm, hbm, hbm],
        out_specs=vmem,
        scratch_shapes=[
            pltpu.VMEM(adjoint_in.shape, f32),
            pltpu.VMEM(courant_lon.shape, f32),
            pltpu.VMEM(courant_lat.shape, f32),
            pltpu.VMEM(innovations.shape, bf16),
            pltpu.VMEM(obs_operator.shape, bf16),
            dma((3,)),
            dma((8,)),
            dma((8,)),
            pltpu.VMEM((nb + 1, 32, 256), f32),
            pltpu.VMEM((1, 128), jnp.int32),
            pltpu.SMEM((1, 128), jnp.int32),
            dma,
            pltpu.VMEM((nz, 128, 256), f32),
            pltpu.VMEM((nz, rest, 256), f32),
            pltpu.VMEM((nz, SPLIT, 256), bf16),
            pltpu.VMEM((nz, SPLIT, 256), bf16),
            dma((2, nz)),
            pltpu.VMEM((2, half, SPLIT, 256), i16),
            pltpu.VMEM((2, half, SPLIT, 256), i16),
            pltpu.VMEM((2, half, 2 * rest, 256), i16),
            pltpu.VMEM((2, half, 2 * rest, 256), i16),
            pltpu.VMEM((4, half, 1, 128), f32),
            pltpu.VMEM((4, half, 1, 128), f32),
            dma((4, half)),
            dma((4, half)),
            dma((4, half)),
            dma((4, half)),
            pltpu.VMEM((rest, 256), i16),
            pltpu.VMEM((rest, 256), i16),
            pltpu.VMEM((1, 128), f32),
            pltpu.VMEM((1, 128), f32),
            dma((2, 2)),
            pltpu.VMEM((STEPS + 1, 4, 4, 8, 256), f32),
            pltpu.VMEM((STEPS, 4, 8, 256), f32),
            pltpu.VMEM((STEPS, 4, 8, 256), f32),
            pltpu.VMEM((STEPS, 4, 8, 256), f32),
            pltpu.VMEM((STEPS, 4, 8, 256), f32),
            pltpu.VMEM((8, 256), f32),
            pltpu.VMEM((8, 256), f32),
            pltpu.VMEM((STEPS, 2, 8, 128), f32),
            pltpu.VMEM((STEPS, 2, 8, 128), f32),
            dma((6, STEPS)),
            dma((6, STEPS)),
            dma((2,)),
            pltpu.VMEM((128, 128), f32),
            pltpu.VMEM((128, 128), f32),
        ],
        compiler_params=pltpu.CompilerParams(
            collective_id=0, has_side_effects=True, vmem_limit_bytes=60 * 2**20
        ),
        name="adjoint",
    )(
        vert_diff,
        horiz_diff,
        block_row,
        obs_count,
        owner_tile.reshape(1, nb),
        adjoint_in,
        courant_lon,
        courant_lat,
        innovations,
        obs_operator,
    )
    return out.reshape(4, 4, 8, 256).transpose(2, 1, 0, 3)


def solution(mesh):
    in_specs = (
        P(None, "lev", "lat", "lon"),
        P("lev", "lat", "lon"),
        P("lev", "lat", "lon"),
        P(),
        P(),
        P(("lon", "lat"), None, "lev", None),
        P(("lon", "lat"), None, None),
        P(("lon", "lat"), None),
        P(("lon", "lat")),
        P(("lon", "lat")),
    )
    out_specs = P(None, "lev", "lat", "lon")
    return jax.shard_map(
        on_device, mesh=mesh, in_specs=in_specs, out_specs=out_specs, check_vma=False
    )
```

```python
import functools

import jax
import jax.numpy as jnp
from jax import lax
from jax.experimental import pallas as pl
from jax.experimental.pallas import tpu as pltpu
from jax.sharding import PartitionSpec as P

STEPS = 3
CAP = 4
TOP = 32000.0
MESH = pl.DeviceIdType.MESH
F32 = jnp.float32


def side(reach):
    parents = {p: p - 1 for p in range(1, min(reach, 3) + 1)}
    if reach > 3:
        collector = (reach + 4) // 2
        parents |= {p: p + 1 for p in range(4, collector)}
        parents |= {p: p - 1 for p in range(collector + 1, reach + 1)}
        parents[collector] = 0
    return parents


def tree(nz):
    parents = side(nz // 2)
    parents |= {-p: -q for p, q in side(nz // 2 - 1).items()}
    best = [8, -7, 3, -3, 4, 7, -6, 5, -4, 2, -2, 6, -5, 1, -1, 0]
    order = [p for p in best if p in parents or p == 0]
    return parents, order


def encode(x):
    rows = x.shape[0]
    peak = jnp.max(jnp.abs(x).reshape(rows // 8, 8, 256), axis=0)
    peak = jnp.maximum(peak[:, :128], peak[:, 128:])
    peak = jnp.maximum(jnp.max(peak, axis=0, keepdims=True), 1e-30)
    gain = TOP / peak
    gain = jnp.concatenate([gain, gain], axis=1)
    return jnp.round(x * gain).astype(jnp.int32).astype(jnp.int16), peak * (1.0 / TOP)


def decode(ints, scale):
    scale = jnp.concatenate([scale, scale], axis=1)
    return ints.astype(jnp.int32).astype(F32) * scale


def kernel(
    sizes,
    vd_s,
    hd_s,
    row_s,
    count_s,
    own_ref,
    adj_hbm,
    cu_hbm,
    cv_hbm,
    inn_hbm,
    op_hbm,
    out_ref,
    adj_ref,
    cu_ref,
    cv_ref,
    inn_ref,
    ops,
    in_sems,
    inn_sem,
    op_sem,
    prod,
    code_v,
    code_s,
    code_sem,
    mine,
    ysend,
    yrecv,
    y_sems,
    zsend,
    zrecv,
    scale_send,
    scale_recv,
    z_sems,
    scale_sems,
    fields,
    lev_lo,
    lev_hi,
    lat_lo,
    lat_hi,
    wind_send,
    wind_recv,
    lon_send,
    lon_recv,
    halo_send_sem,
    halo_recv_sem,
    wind_sems,
    total_lo,
    total_hi,
):
    n_lon, n_lat, n_lev = sizes
    nz = n_lon // 2
    parents, order = tree(nz)
    nb = prod.shape[0] - 1
    lon, lat, lev = (lax.axis_index(name) for name in ("lon", "lat", "lev"))
    z, yl = lon // 2, lon % 2
    partner = z * 2 + (1 - yl)
    sigma = 1 - 2 * (lev % 2)

    def line(offset):
        return ((z + nz + sigma * offset) % nz) * 2 + yl

    east, west = (lon + 1) % n_lon, (lon + n_lon - 1) % n_lon

    groups = op_sem.shape[0]
    per = nb // groups

    def fetch(g):
        part = pl.ds(g * per, per)
        return (
            pltpu.make_async_copy(inn_hbm.at[part], inn_ref.at[part], inn_sem.at[g]),
            pltpu.make_async_copy(op_hbm.at[part], ops.at[part], op_sem.at[g]),
        )

    state = [
        pltpu.make_async_copy(src, dst, in_sems.at[q])
        for q, (src, dst) in enumerate(((adj_hbm, adj_ref), (cu_hbm, cu_ref), (cv_hbm, cv_ref)))
    ]
    for g in range(groups):
        for copy in fetch(g):
            copy.start()
    for copy in state:
        copy.start()

    barrier = pltpu.get_barrier_semaphore()
    offsets = {parent - p for p, parent in parents.items()}
    offsets |= {-offset for offset in offsets}
    greet = [{"lon": line(offset)} for offset in sorted(offsets)]
    greet += [{"lon": east}, {"lon": west}]
    greet += [{"lat": (lat + 1) % n_lat}, {"lat": (lat + n_lat - 1) % n_lat}]
    greet += [{"lev": (lev + 1) % n_lev}, {"lev": (lev + n_lev - 1) % n_lev}]
    for target in greet:
        pl.semaphore_signal(barrier, inc=1, device_id=target, device_id_type=MESH)

    bi = lax.broadcasted_iota(jnp.int32, (nb, nb), 0)
    bj = lax.broadcasted_iota(jnp.int32, (nb, nb), 1)
    trow = own_ref[...]
    tcol = jnp.sum(jnp.where(bi == bj, trow, 0).astype(F32), axis=1, keepdims=True)
    tcol = tcol.astype(jnp.int32)
    earlier = jnp.where((tcol == trow) & (bj < bi), 1.0, 0.0)
    place = jnp.sum(earlier, axis=1, keepdims=True).astype(jnp.int32)
    slot = lax.broadcasted_iota(jnp.int32, (nb, 128), 1)
    number = lax.broadcasted_iota(jnp.int32, (nb, 128), 0)
    hit = (tcol == slot // CAP) & (place == slot % CAP)
    code_v[...] = jnp.sum(jnp.where(hit, number - nb, 0), axis=0, keepdims=True) + nb
    to_smem = pltpu.make_async_copy(code_v, code_s, code_sem)
    to_smem.start()

    prod[nb] = jnp.zeros_like(prod[nb])
    obs = ops.shape[1]
    observation = lax.broadcasted_iota(jnp.int32, (32, obs), 1)

    def multiply(g, carry):
        for copy in fetch(g):
            copy.wait()
        for i in range(per):
            b = g * per + i
            seen = inn_ref[b].astype(F32).reshape(32, obs)
            seen = jnp.where(observation < count_s[b], seen, 0.0).astype(jnp.bfloat16)
            p = jnp.dot(seen, ops[b], preferred_element_type=F32)
            prod[b] = p.astype(jnp.bfloat16).astype(F32)
        return carry

    lax.fori_loop(0, groups, multiply, 0)

    for copy in state:
        copy.wait()
    for j in range(4):
        for k in range(4):
            fields[0, j, k] = adj_ref[:, k, j, :]
    u_first = jnp.concatenate(
        [
            jnp.broadcast_to(cu_ref[k, pl.ds(j, 1), 0:128], (8, 128))
            for j in range(4)
            for k in range(4)
        ],
        axis=0,
    ).T[0:1]
    wind_send[...] = jnp.zeros_like(wind_send)
    for k in range(4):
        wind_send[pl.ds(k, 1)] = cv_ref[k, pl.ds(0, 1), :]
    at_south, at_north = lat == 0, lat == n_lat - 1
    at_low, at_high = lev == 0, lev == n_lev - 1

    @pl.when(at_south)
    def _():
        lat_lo[...] = jnp.zeros_like(lat_lo)

    @pl.when(at_north)
    def _():
        lat_hi[...] = jnp.zeros_like(lat_hi)
        wind_recv[...] = jnp.zeros_like(wind_recv)

    @pl.when(at_low)
    def _():
        lev_lo[...] = jnp.zeros_like(lev_lo)

    @pl.when(at_high)
    def _():
        lev_hi[...] = jnp.zeros_like(lev_hi)

    pl.semaphore_wait(barrier, len(greet))

    def halo(r):
        def copy(q, src, dst, target):
            return pltpu.make_async_remote_copy(
                src_ref=src,
                dst_ref=dst,
                send_sem=halo_send_sem.at[q, r],
                recv_sem=halo_recv_sem.at[q, r],
                device_id=target,
                device_id_type=MESH,
            )

        return (
            copy(0, fields.at[r, 3], lat_lo.at[r], {"lat": (lat + 1) % n_lat}),
            copy(1, fields.at[r, 0], lat_hi.at[r], {"lat": (lat + n_lat - 1) % n_lat}),
            copy(2, fields.at[r, :, 3], lev_lo.at[r], {"lev": (lev + 1) % n_lev}),
            copy(3, fields.at[r, :, 0], lev_hi.at[r], {"lev": (lev + n_lev - 1) % n_lev}),
            copy(4, lon_send.at[r, 0], lon_recv.at[r, 0], {"lon": east}),
            copy(5, lon_send.at[r, 1], lon_recv.at[r, 1], {"lon": west}),
        )

    wind = pltpu.make_async_remote_copy(
        src_ref=wind_send,
        dst_ref=wind_recv,
        send_sem=wind_sems.at[0],
        recv_sem=wind_sems.at[1],
        device_id={"lat": (lat + n_lat - 1) % n_lat},
        device_id_type=MESH,
    )
    sends = (~at_north, ~at_south, ~at_high, ~at_low, None, None)
    arrives = (~at_south, ~at_north, ~at_low, ~at_high, None, None)

    def gated(flag, action):
        if flag is None:
            action()
        else:
            pl.when(flag)(action)

    def send_halo(r):
        flat = fields[r].reshape(128, 256)
        first = flat[:, 0:128].T[0:1]
        last = flat[:, 128:256].T[127:128]
        lon_send[r, 0, pl.ds(0, 1)] = last
        lon_send[r, 1, pl.ds(0, 1)] = first
        lon_send[r, 1, pl.ds(1, 1)] = first * u_first
        for flag, copy in zip(sends, halo(r)):
            gated(flag, copy.start)

    lon_send[...] = jnp.zeros_like(lon_send)
    send_halo(0)
    gated(sends[1], wind.start)

    lane = lax.broadcasted_iota(jnp.int32, (8, 256), 1)
    field = lax.broadcasted_iota(jnp.int32, (8, 256), 0)
    gain = jnp.zeros((8, 256), F32)
    for f in range(8):
        gain = jnp.where(field == f, hd_s[f], gain)

    def sub_step(r):
        for flag, copy in zip(arrives, halo(r)):
            gated(flag, copy.wait_recv)
        edges = jnp.concatenate([lon_recv[r, 0], lon_recv[r, 1]], axis=0).T

        def at(j, k):
            if j < 0:
                return lat_lo[r, k]
            if j > 3:
                return lat_hi[r, k]
            if k < 0:
                return lev_lo[r, j]
            if k > 3:
                return lev_hi[r, j]
            return fields[r, j, k]

        def north_wind(j, k):
            return wind_recv[pl.ds(k, 1)] if j > 3 else cv_ref[k, pl.ds(j, 1), :]

        for k in range(4):
            level = lev * 4 + k
            up = jnp.where(level < n_lev * 4 - 1, vd_s[level], 0.0)
            down = jnp.where(level > 0, vd_s[jnp.maximum(level - 1, 0)], 0.0)
            for j in range(4):
                a = at(j, k)
                rows = slice((j * 4 + k) * 8, (j * 4 + k) * 8 + 8)
                flux = cu_ref[k, pl.ds(j, 1), :] * a
                north_flux = cv_ref[k, pl.ds(j, 1), :] * a
                north, south = at(j + 1, k), at(j - 1, k)
                a_east = jnp.where(lane == 255, edges[rows, 8:9], pltpu.roll(a, 255, 1))
                a_west = jnp.where(lane == 0, edges[rows, 0:1], pltpu.roll(a, 1, 1))
                moved = jnp.where(lane == 255, edges[rows, 9:10], pltpu.roll(flux, 255, 1))
                res = a - flux - north_flux + moved + north_wind(j + 1, k) * north
                res = res + gain * (a_east + a_west + north + south - 4.0 * a)
                res = res + up * (at(j, k + 1) - a)
                res = res + down * (at(j, k - 1) - a)
                fields[r + 1, j, k] = res

    def full_step(r):
        if r == 0:
            gated(arrives[1], wind.wait_recv)
        sub_step(r)
        if r < STEPS - 1:
            send_halo(r + 1)

    to_smem.wait()

    def tile_sum(tile):
        rows = [jnp.zeros((32, 256), F32) for j in range(4)]
        for c in range(CAP):
            b = code_s[0, tile * CAP + c]
            row = row_s[jnp.minimum(b, nb - 1)]
            p = prod[b]
            for j in range(4):
                rows[j] = rows[j] + p * jnp.where(row == j, 1.0, 0.0)
        return jnp.concatenate(rows, axis=0)

    def ycopy(n):
        return pltpu.make_async_remote_copy(
            src_ref=ysend.at[n],
            dst_ref=yrecv.at[n],
            send_sem=y_sems.at[0, n],
            recv_sem=y_sems.at[1, n],
            device_id={"lon": partner},
            device_id_type=MESH,
        )

    def gather(i, carry):
        place = 0
        for c, p in enumerate(order):
            place = jnp.where(i == c, p, place)
        dest = (z + nz - sigma * place) % nz
        ysend[i] = tile_sum(dest * 2 + (1 - yl)).astype(jnp.bfloat16)
        ycopy(i).start()
        mine[i] = tile_sum(dest * 2 + yl)
        return carry

    lax.fori_loop(0, nz, gather, 0)

    def zcopies(i):
        p = order[i]
        target = {"lon": line(parents[p] - p)}
        return [
            pltpu.make_async_remote_copy(
                src_ref=src.at[i],
                dst_ref=dst.at[i],
                send_sem=sems.at[0, i],
                recv_sem=sems.at[1, i],
                device_id=target,
                device_id_type=MESH,
            )
            for src, dst, sems in (
                (zsend, zrecv, z_sems),
                (scale_send, scale_recv, scale_sems),
            )
        ]

    def collect(i):
        ycopy(i).wait_recv()
        x = mine[i] + yrecv[i].astype(F32)
        for child, p in enumerate(order):
            if parents.get(p) == order[i] and p != 0:
                for copy in zcopies(child):
                    copy.wait_recv()
                x = x + decode(zrecv[child], scale_recv[child])
        return x

    due = {2: 0, 6: 1, 10: 2} if nz == 16 else {0: 0, 1: 1, 2: 2}
    for i in range(nz - 1):
        zsend[i], scale_send[i] = encode(collect(i))
        for copy in zcopies(i):
            copy.start()
        if i in due:
            full_step(due[i])

    total = collect(nz - 1)
    total_lo[...], total_hi[...] = total[:, :128], total[:, 128:]
    for j in range(4):
        for k in range(4):
            pick = pl.ds(j * 32 + k, 8, stride=4)
            here = jnp.concatenate([total_lo[pick, :], total_hi[pick, :]], axis=1)
            out_ref[pl.ds((j * 4 + k) * 8, 8)] = fields[STEPS, j, k] + here

    def y_left(n, carry):
        ycopy(n).wait_send()
        return carry

    lax.fori_loop(0, nz, y_left, 0)

    for i in range(nz - 1):
        for copy in zcopies(i):
            copy.wait_send()
    gated(sends[1], wind.wait_send)

    def halo_left(r, carry):
        for flag, copy in zip(sends, halo(r)):
            gated(flag, copy.wait_send)
        return carry

    lax.fori_loop(0, STEPS, halo_left, 0)


def on_device(
    adjoint_in,
    courant_lon,
    courant_lat,
    horiz_diff,
    vert_diff,
    innovations,
    obs_operator,
    owner_tile,
    block_row,
    obs_count,
):
    nb = innovations.shape[0]
    sizes = tuple(lax.axis_size(name) for name in ("lon", "lat", "lev"))
    nz = sizes[0] // 2

    vmem = pl.BlockSpec(memory_space=pltpu.VMEM)
    smem = pl.BlockSpec(memory_space=pltpu.SMEM)
    hbm = pl.BlockSpec(memory_space=pltpu.HBM)
    dma = pltpu.SemaphoreType.DMA
    i16, bf16, f32 = jnp.int16, jnp.bfloat16, jnp.float32
    out = pl.pallas_call(
        functools.partial(kernel, sizes),
        out_shape=jax.ShapeDtypeStruct((128, 256), f32),
        in_specs=[smem, smem, smem, smem, vmem, hbm, hbm, hbm, hbm, hbm],
        out_specs=vmem,
        scratch_shapes=[
            pltpu.VMEM(adjoint_in.shape, f32),
            pltpu.VMEM(courant_lon.shape, f32),
            pltpu.VMEM(courant_lat.shape, f32),
            pltpu.VMEM(innovations.shape, bf16),
            pltpu.VMEM(obs_operator.shape, bf16),
            dma((3,)),
            dma((8,)),
            dma((8,)),
            pltpu.VMEM((nb + 1, 32, 256), f32),
            pltpu.VMEM((1, 128), jnp.int32),
            pltpu.SMEM((1, 128), jnp.int32),
            dma,
            pltpu.VMEM((nz, 128, 256), f32),
            pltpu.VMEM((nz, 128, 256), bf16),
            pltpu.VMEM((nz, 128, 256), bf16),
            dma((2, nz)),
            pltpu.VMEM((nz - 1, 128, 256), i16),
            pltpu.VMEM((nz - 1, 128, 256), i16),
            pltpu.VMEM((nz - 1, 1, 128), f32),
            pltpu.VMEM((nz - 1, 1, 128), f32),
            dma((2, nz - 1)),
            dma((2, nz - 1)),
            pltpu.VMEM((STEPS + 1, 4, 4, 8, 256), f32),
            pltpu.VMEM((STEPS, 4, 8, 256), f32),
            pltpu.VMEM((STEPS, 4, 8, 256), f32),
            pltpu.VMEM((STEPS, 4, 8, 256), f32),
            pltpu.VMEM((STEPS, 4, 8, 256), f32),
            pltpu.VMEM((8, 256), f32),
            pltpu.VMEM((8, 256), f32),
            pltpu.VMEM((STEPS, 2, 8, 128), f32),
            pltpu.VMEM((STEPS, 2, 8, 128), f32),
            dma((6, STEPS)),
            dma((6, STEPS)),
            dma((2,)),
            pltpu.VMEM((128, 128), f32),
            pltpu.VMEM((128, 128), f32),
        ],
        compiler_params=pltpu.CompilerParams(
            collective_id=0, has_side_effects=True, vmem_limit_bytes=60 * 2**20
        ),
        name="adjoint",
    )(
        vert_diff,
        horiz_diff,
        block_row,
        obs_count,
        owner_tile.reshape(1, nb),
        adjoint_in,
        courant_lon,
        courant_lat,
        innovations,
        obs_operator,
    )
    return out.reshape(4, 4, 8, 256).transpose(2, 1, 0, 3)


def solution(mesh):
    in_specs = (
        P(None, "lev", "lat", "lon"),
        P("lev", "lat", "lon"),
        P("lev", "lat", "lon"),
        P(),
        P(),
        P(("lon", "lat"), None, "lev", None),
        P(("lon", "lat"), None, None),
        P(("lon", "lat"), None),
        P(("lon", "lat")),
        P(("lon", "lat")),
    )
    out_specs = P(None, "lev", "lat", "lon")
    return jax.shard_map(
        on_device, mesh=mesh, in_specs=in_specs, out_specs=out_specs, check_vma=False
    )
```

```python
import functools

import jax
import jax.numpy as jnp
from jax import lax
from jax.experimental import pallas as pl
from jax.experimental.pallas import tpu as pltpu
from jax.sharding import PartitionSpec as P

STEPS = 3
CAP = 4
TOP = 32000.0
MESH = pl.DeviceIdType.MESH
F32 = jnp.float32


def side(reach):
    parents = {p: p - 1 for p in range(1, min(reach, 3) + 1)}
    if reach > 3:
        collector = (reach + 4) // 2
        parents |= {p: p + 1 for p in range(4, collector)}
        parents |= {p: p - 1 for p in range(collector + 1, reach + 1)}
        parents[collector] = 0
    return parents


def tree(nz):
    parents = side(nz // 2)
    parents |= {-p: -q for p, q in side(nz // 2 - 1).items()}
    leaves = [p for p, q in parents.items() if p not in parents.values() and abs(p) > abs(q)]
    leaves.sort(key=abs, reverse=True)
    best = [4, -4, 5, 7, -6, 6, -5, 2, -2, 1, -1, 0]
    order = leaves + [p for p in best if p not in leaves and (p in parents or p == 0)]
    return parents, leaves, order


def encode(x):
    rows = x.shape[0]
    peak = jnp.max(jnp.abs(x).reshape(rows // 8, 8, 256), axis=0)
    peak = jnp.maximum(peak[:, :128], peak[:, 128:])
    peak = jnp.maximum(jnp.max(peak, axis=0, keepdims=True), 1e-30)
    gain = TOP / peak
    gain = jnp.concatenate([gain, gain], axis=1)
    return jnp.round(x * gain).astype(jnp.int32).astype(jnp.int16), peak * (1.0 / TOP)


def decode(ints, scale):
    scale = jnp.concatenate([scale, scale], axis=1)
    return ints.astype(jnp.int32).astype(F32) * scale


def kernel(
    sizes,
    vd_s,
    hd_s,
    row_s,
    count_s,
    own_ref,
    adj_hbm,
    cu_hbm,
    cv_hbm,
    inn_hbm,
    op_hbm,
    out_ref,
    adj_ref,
    cu_ref,
    cv_ref,
    inn_ref,
    ops,
    in_sems,
    inn_sem,
    op_sem,
    prod,
    code_v,
    code_s,
    code_sem,
    mine,
    theirs,
    lsend,
    lrecv,
    ysend,
    yrecv,
    y_sems,
    zsend,
    zrecv,
    scale_send,
    scale_recv,
    z_sems,
    scale_sems,
    fields,
    lev_lo,
    lev_hi,
    lat_lo,
    lat_hi,
    wind_send,
    wind_recv,
    lon_send,
    lon_recv,
    halo_send_sem,
    halo_recv_sem,
    wind_sems,
    total_lo,
    total_hi,
):
    n_lon, n_lat, n_lev = sizes
    nz = n_lon // 2
    parents, leaves, order = tree(nz)
    nl = len(leaves)
    nb = prod.shape[0] - 1
    lon, lat, lev = (lax.axis_index(name) for name in ("lon", "lat", "lev"))
    z, yl = lon // 2, lon % 2
    partner = z * 2 + (1 - yl)
    sigma = 1 - 2 * (lev % 2)

    def line(offset):
        return ((z + nz + sigma * offset) % nz) * 2 + yl

    east, west = (lon + 1) % n_lon, (lon + n_lon - 1) % n_lon

    groups = op_sem.shape[0]
    per = nb // groups

    def fetch(g):
        part = pl.ds(g * per, per)
        return (
            pltpu.make_async_copy(inn_hbm.at[part], inn_ref.at[part], inn_sem.at[g]),
            pltpu.make_async_copy(op_hbm.at[part], ops.at[part], op_sem.at[g]),
        )

    state = [
        pltpu.make_async_copy(src, dst, in_sems.at[q])
        for q, (src, dst) in enumerate(((adj_hbm, adj_ref), (cu_hbm, cu_ref), (cv_hbm, cv_ref)))
    ]
    for g in range(groups):
        for copy in fetch(g):
            copy.start()
    for copy in state:
        copy.start()

    barrier = pltpu.get_barrier_semaphore()
    offsets = {parent - p for p, parent in parents.items()}
    offsets |= {-offset for offset in offsets}
    greet = [{"lon": line(offset)} for offset in sorted(offsets)]
    greet += [{"lon": east}, {"lon": west}]
    greet += [{"lat": (lat + 1) % n_lat}, {"lat": (lat + n_lat - 1) % n_lat}]
    greet += [{"lev": (lev + 1) % n_lev}, {"lev": (lev + n_lev - 1) % n_lev}]
    for target in greet:
        pl.semaphore_signal(barrier, inc=1, device_id=target, device_id_type=MESH)

    bi = lax.broadcasted_iota(jnp.int32, (nb, nb), 0)
    bj = lax.broadcasted_iota(jnp.int32, (nb, nb), 1)
    trow = own_ref[...]
    tcol = jnp.sum(jnp.where(bi == bj, trow, 0).astype(F32), axis=1, keepdims=True)
    tcol = tcol.astype(jnp.int32)
    earlier = jnp.where((tcol == trow) & (bj < bi), 1.0, 0.0)
    place = jnp.sum(earlier, axis=1, keepdims=True).astype(jnp.int32)
    slot = lax.broadcasted_iota(jnp.int32, (nb, 128), 1)
    number = lax.broadcasted_iota(jnp.int32, (nb, 128), 0)
    hit = (tcol == slot // CAP) & (place == slot % CAP)
    code_v[...] = jnp.sum(jnp.where(hit, number - nb, 0), axis=0, keepdims=True) + nb
    to_smem = pltpu.make_async_copy(code_v, code_s, code_sem)
    to_smem.start()

    prod[nb] = jnp.zeros_like(prod[nb])
    obs = ops.shape[1]
    observation = lax.broadcasted_iota(jnp.int32, (32, obs), 1)

    def multiply(g, carry):
        for copy in fetch(g):
            copy.wait()
        for i in range(per):
            b = g * per + i
            seen = inn_ref[b].astype(F32).reshape(32, obs)
            seen = jnp.where(observation < count_s[b], seen, 0.0).astype(jnp.bfloat16)
            p = jnp.dot(seen, ops[b], preferred_element_type=F32)
            prod[b] = p.astype(jnp.bfloat16).astype(F32)
        return carry

    lax.fori_loop(0, groups, multiply, 0)

    for copy in state:
        copy.wait()
    for j in range(4):
        for k in range(4):
            fields[0, j, k] = adj_ref[:, k, j, :]
    u_first = jnp.concatenate(
        [
            jnp.broadcast_to(cu_ref[k, pl.ds(j, 1), 0:128], (8, 128))
            for j in range(4)
            for k in range(4)
        ],
        axis=0,
    ).T[0:1]
    wind_send[...] = jnp.zeros_like(wind_send)
    for k in range(4):
        wind_send[pl.ds(k, 1)] = cv_ref[k, pl.ds(0, 1), :]
    at_south, at_north = lat == 0, lat == n_lat - 1
    at_low, at_high = lev == 0, lev == n_lev - 1

    @pl.when(at_south)
    def _():
        lat_lo[...] = jnp.zeros_like(lat_lo)

    @pl.when(at_north)
    def _():
        lat_hi[...] = jnp.zeros_like(lat_hi)
        wind_recv[...] = jnp.zeros_like(wind_recv)

    @pl.when(at_low)
    def _():
        lev_lo[...] = jnp.zeros_like(lev_lo)

    @pl.when(at_high)
    def _():
        lev_hi[...] = jnp.zeros_like(lev_hi)

    pl.semaphore_wait(barrier, len(greet))

    def halo(r):
        def copy(q, src, dst, target):
            return pltpu.make_async_remote_copy(
                src_ref=src,
                dst_ref=dst,
                send_sem=halo_send_sem.at[q, r],
                recv_sem=halo_recv_sem.at[q, r],
                device_id=target,
                device_id_type=MESH,
            )

        return (
            copy(0, fields.at[r, 3], lat_lo.at[r], {"lat": (lat + 1) % n_lat}),
            copy(1, fields.at[r, 0], lat_hi.at[r], {"lat": (lat + n_lat - 1) % n_lat}),
            copy(2, fields.at[r, :, 3], lev_lo.at[r], {"lev": (lev + 1) % n_lev}),
            copy(3, fields.at[r, :, 0], lev_hi.at[r], {"lev": (lev + n_lev - 1) % n_lev}),
            copy(4, lon_send.at[r, 0], lon_recv.at[r, 0], {"lon": east}),
            copy(5, lon_send.at[r, 1], lon_recv.at[r, 1], {"lon": west}),
        )

    wind = pltpu.make_async_remote_copy(
        src_ref=wind_send,
        dst_ref=wind_recv,
        send_sem=wind_sems.at[0],
        recv_sem=wind_sems.at[1],
        device_id={"lat": (lat + n_lat - 1) % n_lat},
        device_id_type=MESH,
    )
    sends = (~at_north, ~at_south, ~at_high, ~at_low, None, None)
    arrives = (~at_south, ~at_north, ~at_low, ~at_high, None, None)

    def gated(flag, action):
        if flag is None:
            action()
        else:
            pl.when(flag)(action)

    def send_halo(r):
        flat = fields[r].reshape(128, 256)
        first = flat[:, 0:128].T[0:1]
        last = flat[:, 128:256].T[127:128]
        lon_send[r, 0, pl.ds(0, 1)] = last
        lon_send[r, 1, pl.ds(0, 1)] = first
        lon_send[r, 1, pl.ds(1, 1)] = first * u_first
        for flag, copy in zip(sends, halo(r)):
            gated(flag, copy.start)

    lon_send[...] = jnp.zeros_like(lon_send)
    send_halo(0)
    gated(sends[1], wind.start)

    lane = lax.broadcasted_iota(jnp.int32, (8, 256), 1)
    field = lax.broadcasted_iota(jnp.int32, (8, 256), 0)
    gain = jnp.zeros((8, 256), F32)
    for f in range(8):
        gain = jnp.where(field == f, hd_s[f], gain)

    def sub_step(r):
        for flag, copy in zip(arrives, halo(r)):
            gated(flag, copy.wait_recv)
        edges = jnp.concatenate([lon_recv[r, 0], lon_recv[r, 1]], axis=0).T

        def at(j, k):
            if j < 0:
                return lat_lo[r, k]
            if j > 3:
                return lat_hi[r, k]
            if k < 0:
                return lev_lo[r, j]
            if k > 3:
                return lev_hi[r, j]
            return fields[r, j, k]

        def north_wind(j, k):
            return wind_recv[pl.ds(k, 1)] if j > 3 else cv_ref[k, pl.ds(j, 1), :]

        for k in range(4):
            level = lev * 4 + k
            up = jnp.where(level < n_lev * 4 - 1, vd_s[level], 0.0)
            down = jnp.where(level > 0, vd_s[jnp.maximum(level - 1, 0)], 0.0)
            for j in range(4):
                a = at(j, k)
                rows = slice((j * 4 + k) * 8, (j * 4 + k) * 8 + 8)
                flux = cu_ref[k, pl.ds(j, 1), :] * a
                north_flux = cv_ref[k, pl.ds(j, 1), :] * a
                north, south = at(j + 1, k), at(j - 1, k)
                a_east = jnp.where(lane == 255, edges[rows, 8:9], pltpu.roll(a, 255, 1))
                a_west = jnp.where(lane == 0, edges[rows, 0:1], pltpu.roll(a, 1, 1))
                moved = jnp.where(lane == 255, edges[rows, 9:10], pltpu.roll(flux, 255, 1))
                res = a - flux - north_flux + moved + north_wind(j + 1, k) * north
                res = res + gain * (a_east + a_west + north + south - 4.0 * a)
                res = res + up * (at(j, k + 1) - a)
                res = res + down * (at(j, k - 1) - a)
                fields[r + 1, j, k] = res

    def full_step(r):
        if r == 0:
            gated(arrives[1], wind.wait_recv)
        sub_step(r)
        if r < STEPS - 1:
            send_halo(r + 1)

    to_smem.wait()

    def tile_sum(tile):
        rows = [jnp.zeros((32, 256), F32) for j in range(4)]
        for c in range(CAP):
            b = code_s[0, tile * CAP + c]
            row = row_s[jnp.minimum(b, nb - 1)]
            p = prod[b]
            for j in range(4):
                rows[j] = rows[j] + p * jnp.where(row == j, 1.0, 0.0)
        return jnp.concatenate(rows, axis=0)

    def gather(i, carry):
        place = 0
        for c, p in enumerate(order):
            place = jnp.where(i == c, p, place)
        dest = (z + nz - sigma * place) % nz
        mine[i] = tile_sum(dest * 2 + yl)
        theirs[i] = tile_sum(dest * 2 + (1 - yl))
        return carry

    def ycopy(i):
        return pltpu.make_async_remote_copy(
            src_ref=ysend.at[i - nl],
            dst_ref=yrecv.at[i - nl],
            send_sem=y_sems.at[0, i - nl],
            recv_sem=y_sems.at[1, i - nl],
            device_id={"lon": partner},
            device_id_type=MESH,
        )

    def zcopies(i):
        p = order[i]
        target = {"lon": line(parents[p] - p)}
        if i < nl:
            data = (lsend.at[i], lrecv.at[i], z_sems)
        else:
            data = (zsend.at[i - nl], zrecv.at[i - nl], z_sems)
        return [
            pltpu.make_async_remote_copy(
                src_ref=src,
                dst_ref=dst,
                send_sem=sems.at[0, i],
                recv_sem=sems.at[1, i],
                device_id=target,
                device_id_type=MESH,
            )
            for src, dst, sems in (data, (scale_send.at[i], scale_recv.at[i], scale_sems))
        ]

    def children(i):
        return [c for c, p in enumerate(order) if p != 0 and parents[p] == order[i]]

    def cross(i):
        x = theirs[i]
        for child in children(i):
            if child < nl:
                for copy in zcopies(child):
                    copy.wait_recv()
                x = x + decode(lrecv[child, 128:], scale_recv[child])
        ysend[i - nl] = x.astype(jnp.bfloat16)
        ycopy(i).start()

    def collect(i):
        ycopy(i).wait_recv()
        x = mine[i] + yrecv[i - nl].astype(F32)
        for child in children(i):
            if child < nl:
                x = x + decode(lrecv[child, :128], scale_recv[child])
            else:
                for copy in zcopies(child):
                    copy.wait_recv()
                x = x + decode(zrecv[child - nl], scale_recv[child])
        return x

    lax.fori_loop(0, nl, gather, 0)
    for i in range(nl):
        lsend[i], scale_send[i] = encode(jnp.concatenate([mine[i], theirs[i]], axis=0))
        for copy in zcopies(i):
            copy.start()
    lax.fori_loop(nl, nz, gather, 0)

    crossed = nl
    due = {nl - 1: 0, nl + 4: 1, nl + 7: 2} if nz == 16 else {nl - 1: 0, nl: 1, nl + 1: 2}
    for i in range(nl - 1, nz - 1):
        if i >= nl:
            zsend[i - nl], scale_send[i] = encode(collect(i))
            for copy in zcopies(i):
                copy.start()
        while crossed < min(nz, i + 4 if i < nl else i + 6):
            cross(crossed)
            crossed += 1
        if i in due:
            full_step(due[i])
    while crossed < nz:
        cross(crossed)
        crossed += 1
    for r in range(STEPS):
        if r not in [due[i] for i in due if i < nz - 1]:
            full_step(r)

    total = collect(nz - 1)
    total_lo[...], total_hi[...] = total[:, :128], total[:, 128:]
    for j in range(4):
        for k in range(4):
            pick = pl.ds(j * 32 + k, 8, stride=4)
            here = jnp.concatenate([total_lo[pick, :], total_hi[pick, :]], axis=1)
            out_ref[pl.ds((j * 4 + k) * 8, 8)] = fields[STEPS, j, k] + here

    for i in range(nl, nz):
        ycopy(i).wait_send()
    for i in range(nz - 1):
        for copy in zcopies(i):
            copy.wait_send()
    gated(sends[1], wind.wait_send)

    def halo_left(r, carry):
        for flag, copy in zip(sends, halo(r)):
            gated(flag, copy.wait_send)
        return carry

    lax.fori_loop(0, STEPS, halo_left, 0)


def on_device(
    adjoint_in,
    courant_lon,
    courant_lat,
    horiz_diff,
    vert_diff,
    innovations,
    obs_operator,
    owner_tile,
    block_row,
    obs_count,
):
    nb = innovations.shape[0]
    sizes = tuple(lax.axis_size(name) for name in ("lon", "lat", "lev"))
    nz = sizes[0] // 2
    nl = len(tree(nz)[1])

    vmem = pl.BlockSpec(memory_space=pltpu.VMEM)
    smem = pl.BlockSpec(memory_space=pltpu.SMEM)
    hbm = pl.BlockSpec(memory_space=pltpu.HBM)
    dma = pltpu.SemaphoreType.DMA
    i16, bf16, f32 = jnp.int16, jnp.bfloat16, jnp.float32
    out = pl.pallas_call(
        functools.partial(kernel, sizes),
        out_shape=jax.ShapeDtypeStruct((128, 256), f32),
        in_specs=[smem, smem, smem, smem, vmem, hbm, hbm, hbm, hbm, hbm],
        out_specs=vmem,
        scratch_shapes=[
            pltpu.VMEM(adjoint_in.shape, f32),
            pltpu.VMEM(courant_lon.shape, f32),
            pltpu.VMEM(courant_lat.shape, f32),
            pltpu.VMEM(innovations.shape, bf16),
            pltpu.VMEM(obs_operator.shape, bf16),
            dma((3,)),
            dma((8,)),
            dma((8,)),
            pltpu.VMEM((nb + 1, 32, 256), f32),
            pltpu.VMEM((1, 128), jnp.int32),
            pltpu.SMEM((1, 128), jnp.int32),
            dma,
            pltpu.VMEM((nz, 128, 256), f32),
            pltpu.VMEM((nz, 128, 256), f32),
            pltpu.VMEM((nl, 256, 256), i16),
            pltpu.VMEM((nl, 256, 256), i16),
            pltpu.VMEM((nz - nl, 128, 256), bf16),
            pltpu.VMEM((nz - nl, 128, 256), bf16),
            dma((2, nz - nl)),
            pltpu.VMEM((nz - nl, 128, 256), i16),
            pltpu.VMEM((nz - nl, 128, 256), i16),
            pltpu.VMEM((nz - 1, 1, 128), f32),
            pltpu.VMEM((nz - 1, 1, 128), f32),
            dma((2, nz - 1)),
            dma((2, nz - 1)),
            pltpu.VMEM((STEPS + 1, 4, 4, 8, 256), f32),
            pltpu.VMEM((STEPS, 4, 8, 256), f32),
            pltpu.VMEM((STEPS, 4, 8, 256), f32),
            pltpu.VMEM((STEPS, 4, 8, 256), f32),
            pltpu.VMEM((STEPS, 4, 8, 256), f32),
            pltpu.VMEM((8, 256), f32),
            pltpu.VMEM((8, 256), f32),
            pltpu.VMEM((STEPS, 2, 8, 128), f32),
            pltpu.VMEM((STEPS, 2, 8, 128), f32),
            dma((6, STEPS)),
            dma((6, STEPS)),
            dma((2,)),
            pltpu.VMEM((128, 128), f32),
            pltpu.VMEM((128, 128), f32),
        ],
        compiler_params=pltpu.CompilerParams(
            collective_id=0, has_side_effects=True, vmem_limit_bytes=60 * 2**20
        ),
        name="adjoint",
    )(
        vert_diff,
        horiz_diff,
        block_row,
        obs_count,
        owner_tile.reshape(1, nb),
        adjoint_in,
        courant_lon,
        courant_lat,
        innovations,
        obs_operator,
    )
    return out.reshape(4, 4, 8, 256).transpose(2, 1, 0, 3)


def solution(mesh):
    in_specs = (
        P(None, "lev", "lat", "lon"),
        P("lev", "lat", "lon"),
        P("lev", "lat", "lon"),
        P(),
        P(),
        P(("lon", "lat"), None, "lev", None),
        P(("lon", "lat"), None, None),
        P(("lon", "lat"), None),
        P(("lon", "lat")),
        P(("lon", "lat")),
    )
    out_specs = P(None, "lev", "lat", "lon")
    return jax.shard_map(
        on_device, mesh=mesh, in_specs=in_specs, out_specs=out_specs, check_vma=False
    )
```

```python
import functools

import jax
import jax.numpy as jnp
from jax import lax
from jax.experimental import pallas as pl
from jax.experimental.pallas import tpu as pltpu
from jax.sharding import PartitionSpec as P

STEPS = 3
CAP = 4
TOP = 32000.0
MESH = pl.DeviceIdType.MESH
F32 = jnp.float32


def side(reach):
    parents = {p: p - 1 for p in range(1, min(reach, 3) + 1)}
    if reach > 3:
        collector = (reach + 4) // 2
        parents |= {p: p + 1 for p in range(4, collector)}
        parents |= {p: p - 1 for p in range(collector + 1, reach + 1)}
        parents[collector] = 0
    return parents


def tree(nz):
    parents = side(nz // 2)
    parents |= {-p: -q for p, q in side(nz // 2 - 1).items()}
    leaves = [p for p, q in parents.items() if p not in parents.values() and abs(p) > abs(q)]
    leaves.sort(key=abs, reverse=True)
    best = [8, -7, 4, -4, 3, -3, 5, 7, -6, 6, -5, 2, -2, 1, -1, 0]
    order = leaves + [p for p in best if p not in leaves and (p in parents or p == 0)]
    return parents, leaves, order


def encode(x):
    rows = x.shape[0]
    peak = jnp.max(jnp.abs(x).reshape(rows // 8, 8, 256), axis=0)
    peak = jnp.maximum(peak[:, :128], peak[:, 128:])
    peak = jnp.maximum(jnp.max(peak, axis=0, keepdims=True), 1e-30)
    gain = TOP / peak
    gain = jnp.concatenate([gain, gain], axis=1)
    return jnp.round(x * gain).astype(jnp.int32).astype(jnp.int16), peak * (1.0 / TOP)


def decode(ints, scale):
    scale = jnp.concatenate([scale, scale], axis=1)
    return ints.astype(jnp.int32).astype(F32) * scale


def kernel(
    sizes,
    vd_hbm,
    hd_hbm,
    row_hbm,
    count_hbm,
    own_hbm,
    adj_hbm,
    cu_hbm,
    cv_hbm,
    inn_hbm,
    op_hbm,
    out_ref,
    vd_s,
    hd_s,
    row_s,
    count_s,
    own_ref,
    adj_ref,
    cu_ref,
    cv_ref,
    inn_ref,
    ops,
    in_sems,
    inn_sem,
    op_sem,
    prod,
    code_v,
    code_s,
    code_sem,
    mine,
    theirs,
    lsend,
    lrecv,
    ysend,
    yrecv,
    y_sems,
    zsend,
    zrecv,
    scale_send,
    scale_recv,
    z_sems,
    scale_sems,
    fields,
    lev_lo,
    lev_hi,
    lat_lo,
    lat_hi,
    wind_send,
    wind_recv,
    lon_send,
    lon_recv,
    halo_send_sem,
    halo_recv_sem,
    wind_sems,
    total_lo,
    total_hi,
):
    n_lon, n_lat, n_lev = sizes
    nz = n_lon // 2
    parents, leaves, order = tree(nz)
    nl = len(leaves)
    nb = prod.shape[0] - 1
    lon, lat, lev = (lax.axis_index(name) for name in ("lon", "lat", "lev"))
    z, yl = lon // 2, lon % 2
    partner = z * 2 + (1 - yl)
    sigma = 1 - 2 * (lev % 2)

    def line(offset):
        return ((z + nz + sigma * offset) % nz) * 2 + yl

    east, west = (lon + 1) % n_lon, (lon + n_lon - 1) % n_lon

    groups = op_sem.shape[0]
    per = nb // groups

    def fetch(g):
        part = pl.ds(g * per, per)
        return (
            pltpu.make_async_copy(inn_hbm.at[part], inn_ref.at[part], inn_sem.at[g]),
            pltpu.make_async_copy(op_hbm.at[part], ops.at[part], op_sem.at[g]),
        )

    inputs = (
        (own_hbm, own_ref),
        (count_hbm, count_s),
        (row_hbm, row_s),
        (vd_hbm, vd_s),
        (hd_hbm, hd_s),
        (adj_hbm, adj_ref),
        (cu_hbm, cu_ref),
        (cv_hbm, cv_ref),
    )
    inputs = [
        pltpu.make_async_copy(src, dst, in_sems.at[q]) for q, (src, dst) in enumerate(inputs)
    ]
    tables, state = inputs[:5], inputs[5:]
    for copy in tables:
        copy.start()
    for g in range(groups):
        for copy in fetch(g):
            copy.start()
    for copy in state:
        copy.start()

    barrier = pltpu.get_barrier_semaphore()
    offsets = {parent - p for p, parent in parents.items()}
    offsets |= {-offset for offset in offsets}
    greet = [{"lon": line(offset)} for offset in sorted(offsets)]
    greet += [{"lon": east}, {"lon": west}]
    greet += [{"lat": (lat + 1) % n_lat}, {"lat": (lat + n_lat - 1) % n_lat}]
    greet += [{"lev": (lev + 1) % n_lev}, {"lev": (lev + n_lev - 1) % n_lev}]
    for target in greet:
        pl.semaphore_signal(barrier, inc=1, device_id=target, device_id_type=MESH)

    for copy in tables:
        copy.wait()

    bi = lax.broadcasted_iota(jnp.int32, (nb, nb), 0)
    bj = lax.broadcasted_iota(jnp.int32, (nb, nb), 1)
    trow = own_ref[...]
    tcol = jnp.sum(jnp.where(bi == bj, trow, 0).astype(F32), axis=1, keepdims=True)
    tcol = tcol.astype(jnp.int32)
    earlier = jnp.where((tcol == trow) & (bj < bi), 1.0, 0.0)
    place = jnp.sum(earlier, axis=1, keepdims=True).astype(jnp.int32)
    slot = lax.broadcasted_iota(jnp.int32, (nb, 128), 1)
    number = lax.broadcasted_iota(jnp.int32, (nb, 128), 0)
    hit = (tcol == slot // CAP) & (place == slot % CAP)
    code_v[...] = jnp.sum(jnp.where(hit, number - nb, 0), axis=0, keepdims=True) + nb
    to_smem = pltpu.make_async_copy(code_v, code_s, code_sem)
    to_smem.start()

    prod[nb] = jnp.zeros_like(prod[nb])
    obs = ops.shape[1]
    observation = lax.broadcasted_iota(jnp.int32, (32, obs), 1)

    def multiply(g, carry):
        for copy in fetch(g):
            copy.wait()
        for i in range(per):
            b = g * per + i
            seen = inn_ref[b].astype(F32).reshape(32, obs)
            seen = jnp.where(observation < count_s[b], seen, 0.0).astype(jnp.bfloat16)
            p = jnp.dot(seen, ops[b], preferred_element_type=F32)
            prod[b] = p.astype(jnp.bfloat16).astype(F32)
        return carry

    lax.fori_loop(0, groups, multiply, 0)

    for copy in state:
        copy.wait()
    for j in range(4):
        for k in range(4):
            fields[0, j, k] = adj_ref[:, k, j, :]
    u_first = jnp.concatenate(
        [
            jnp.broadcast_to(cu_ref[k, pl.ds(j, 1), 0:128], (8, 128))
            for j in range(4)
            for k in range(4)
        ],
        axis=0,
    ).T[0:1]
    wind_send[...] = jnp.zeros_like(wind_send)
    for k in range(4):
        wind_send[pl.ds(k, 1)] = cv_ref[k, pl.ds(0, 1), :]
    at_south, at_north = lat == 0, lat == n_lat - 1
    at_low, at_high = lev == 0, lev == n_lev - 1

    @pl.when(at_south)
    def _():
        lat_lo[...] = jnp.zeros_like(lat_lo)

    @pl.when(at_north)
    def _():
        lat_hi[...] = jnp.zeros_like(lat_hi)
        wind_recv[...] = jnp.zeros_like(wind_recv)

    @pl.when(at_low)
    def _():
        lev_lo[...] = jnp.zeros_like(lev_lo)

    @pl.when(at_high)
    def _():
        lev_hi[...] = jnp.zeros_like(lev_hi)

    pl.semaphore_wait(barrier, len(greet))

    def halo(r):
        def copy(q, src, dst, target):
            return pltpu.make_async_remote_copy(
                src_ref=src,
                dst_ref=dst,
                send_sem=halo_send_sem.at[q, r],
                recv_sem=halo_recv_sem.at[q, r],
                device_id=target,
                device_id_type=MESH,
            )

        return (
            copy(0, fields.at[r, 3], lat_lo.at[r], {"lat": (lat + 1) % n_lat}),
            copy(1, fields.at[r, 0], lat_hi.at[r], {"lat": (lat + n_lat - 1) % n_lat}),
            copy(2, fields.at[r, :, 3], lev_lo.at[r], {"lev": (lev + 1) % n_lev}),
            copy(3, fields.at[r, :, 0], lev_hi.at[r], {"lev": (lev + n_lev - 1) % n_lev}),
            copy(4, lon_send.at[r, 0], lon_recv.at[r, 0], {"lon": east}),
            copy(5, lon_send.at[r, 1], lon_recv.at[r, 1], {"lon": west}),
        )

    wind = pltpu.make_async_remote_copy(
        src_ref=wind_send,
        dst_ref=wind_recv,
        send_sem=wind_sems.at[0],
        recv_sem=wind_sems.at[1],
        device_id={"lat": (lat + n_lat - 1) % n_lat},
        device_id_type=MESH,
    )
    sends = (~at_north, ~at_south, ~at_high, ~at_low, None, None)
    arrives = (~at_south, ~at_north, ~at_low, ~at_high, None, None)

    def gated(flag, action):
        if flag is None:
            action()
        else:
            pl.when(flag)(action)

    def send_halo(r):
        flat = fields[r].reshape(128, 256)
        first = flat[:, 0:128].T[0:1]
        last = flat[:, 128:256].T[127:128]
        lon_send[r, 0, pl.ds(0, 1)] = last
        lon_send[r, 1, pl.ds(0, 1)] = first
        lon_send[r, 1, pl.ds(1, 1)] = first * u_first
        for flag, copy in zip(sends, halo(r)):
            gated(flag, copy.start)

    lon_send[...] = jnp.zeros_like(lon_send)
    send_halo(0)
    gated(sends[1], wind.start)

    lane = lax.broadcasted_iota(jnp.int32, (8, 256), 1)
    field = lax.broadcasted_iota(jnp.int32, (8, 256), 0)
    gain = jnp.zeros((8, 256), F32)
    for f in range(8):
        gain = jnp.where(field == f, hd_s[f], gain)

    def sub_step(r):
        for flag, copy in zip(arrives, halo(r)):
            gated(flag, copy.wait_recv)
        edges = jnp.concatenate([lon_recv[r, 0], lon_recv[r, 1]], axis=0).T

        def at(j, k):
            if j < 0:
                return lat_lo[r, k]
            if j > 3:
                return lat_hi[r, k]
            if k < 0:
                return lev_lo[r, j]
            if k > 3:
                return lev_hi[r, j]
            return fields[r, j, k]

        def north_wind(j, k):
            return wind_recv[pl.ds(k, 1)] if j > 3 else cv_ref[k, pl.ds(j, 1), :]

        for k in range(4):
            level = lev * 4 + k
            up = jnp.where(level < n_lev * 4 - 1, vd_s[level], 0.0)
            down = jnp.where(level > 0, vd_s[jnp.maximum(level - 1, 0)], 0.0)
            for j in range(4):
                a = at(j, k)
                rows = slice((j * 4 + k) * 8, (j * 4 + k) * 8 + 8)
                flux = cu_ref[k, pl.ds(j, 1), :] * a
                north_flux = cv_ref[k, pl.ds(j, 1), :] * a
                north, south = at(j + 1, k), at(j - 1, k)
                a_east = jnp.where(lane == 255, edges[rows, 8:9], pltpu.roll(a, 255, 1))
                a_west = jnp.where(lane == 0, edges[rows, 0:1], pltpu.roll(a, 1, 1))
                moved = jnp.where(lane == 255, edges[rows, 9:10], pltpu.roll(flux, 255, 1))
                res = a - flux - north_flux + moved + north_wind(j + 1, k) * north
                res = res + gain * (a_east + a_west + north + south - 4.0 * a)
                res = res + up * (at(j, k + 1) - a)
                res = res + down * (at(j, k - 1) - a)
                fields[r + 1, j, k] = res

    def full_step(r):
        if r == 0:
            gated(arrives[1], wind.wait_recv)
        sub_step(r)
        if r < STEPS - 1:
            send_halo(r + 1)

    to_smem.wait()

    def tile_sum(tile):
        rows = [jnp.zeros((32, 256), F32) for j in range(4)]
        for c in range(CAP):
            b = code_s[0, tile * CAP + c]
            row = row_s[jnp.minimum(b, nb - 1)]
            p = prod[b]
            for j in range(4):
                rows[j] = rows[j] + p * jnp.where(row == j, 1.0, 0.0)
        return jnp.concatenate(rows, axis=0)

    def gather(i, carry):
        place = 0
        for c, p in enumerate(order):
            place = jnp.where(i == c, p, place)
        dest = (z + nz - sigma * place) % nz
        mine[i] = tile_sum(dest * 2 + yl)
        theirs[i] = tile_sum(dest * 2 + (1 - yl))
        return carry

    def ycopy(i):
        return pltpu.make_async_remote_copy(
            src_ref=ysend.at[i - nl],
            dst_ref=yrecv.at[i - nl],
            send_sem=y_sems.at[0, i - nl],
            recv_sem=y_sems.at[1, i - nl],
            device_id={"lon": partner},
            device_id_type=MESH,
        )

    def zcopies(i):
        p = order[i]
        target = {"lon": line(parents[p] - p)}
        if i < nl:
            data = (lsend.at[i], lrecv.at[i], z_sems)
        else:
            data = (zsend.at[i - nl], zrecv.at[i - nl], z_sems)
        return [
            pltpu.make_async_remote_copy(
                src_ref=src,
                dst_ref=dst,
                send_sem=sems.at[0, i],
                recv_sem=sems.at[1, i],
                device_id=target,
                device_id_type=MESH,
            )
            for src, dst, sems in (data, (scale_send.at[i], scale_recv.at[i], scale_sems))
        ]

    def children(i):
        return [c for c, p in enumerate(order) if p != 0 and parents[p] == order[i]]

    def cross(i):
        x = theirs[i]
        for child in children(i):
            if child < nl:
                for copy in zcopies(child):
                    copy.wait_recv()
                x = x + decode(lrecv[child, 128:], scale_recv[child])
        ysend[i - nl] = x.astype(jnp.bfloat16)
        ycopy(i).start()

    def collect(i):
        ycopy(i).wait_recv()
        x = mine[i] + yrecv[i - nl].astype(F32)
        for child in children(i):
            if child < nl:
                x = x + decode(lrecv[child, :128], scale_recv[child])
            else:
                for copy in zcopies(child):
                    copy.wait_recv()
                x = x + decode(zrecv[child - nl], scale_recv[child])
        return x

    lax.fori_loop(0, nl, gather, 0)
    for i in range(nl):
        lsend[i], scale_send[i] = encode(jnp.concatenate([mine[i], theirs[i]], axis=0))
        for copy in zcopies(i):
            copy.start()
    lax.fori_loop(nl, nz, gather, 0)

    crossed = nl
    due = {nl - 1: 0, nl + 4: 1, nl + 7: 2} if nz == 16 else {nl - 1: 0, nl: 1, nl + 1: 2}
    for i in range(nl - 1, nz - 1):
        if i >= nl:
            zsend[i - nl], scale_send[i] = encode(collect(i))
            for copy in zcopies(i):
                copy.start()
        while crossed < min(nz, i + 4 if i < nl else i + 6):
            cross(crossed)
            crossed += 1
        if i in due:
            full_step(due[i])
    while crossed < nz:
        cross(crossed)
        crossed += 1
    for r in range(STEPS):
        if r not in [due[i] for i in due if i < nz - 1]:
            full_step(r)

    total = collect(nz - 1)
    total_lo[...], total_hi[...] = total[:, :128], total[:, 128:]
    for j in range(4):
        for k in range(4):
            pick = pl.ds(j * 32 + k, 8, stride=4)
            here = jnp.concatenate([total_lo[pick, :], total_hi[pick, :]], axis=1)
            out_ref[pl.ds((j * 4 + k) * 8, 8)] = fields[STEPS, j, k] + here

    for i in range(nl, nz):
        ycopy(i).wait_send()
    for i in range(nz - 1):
        for copy in zcopies(i):
            copy.wait_send()
    gated(sends[1], wind.wait_send)

    def halo_left(r, carry):
        for flag, copy in zip(sends, halo(r)):
            gated(flag, copy.wait_send)
        return carry

    lax.fori_loop(0, STEPS, halo_left, 0)


def on_device(
    adjoint_in,
    courant_lon,
    courant_lat,
    horiz_diff,
    vert_diff,
    innovations,
    obs_operator,
    owner_tile,
    block_row,
    obs_count,
):
    nb = innovations.shape[0]
    sizes = tuple(lax.axis_size(name) for name in ("lon", "lat", "lev"))
    nz = sizes[0] // 2
    nl = len(tree(nz)[1])

    vmem = pl.BlockSpec(memory_space=pltpu.VMEM)
    hbm = pl.BlockSpec(memory_space=pltpu.HBM)
    dma = pltpu.SemaphoreType.DMA
    i16, bf16, f32 = jnp.int16, jnp.bfloat16, jnp.float32
    operands = (
        vert_diff,
        horiz_diff,
        block_row,
        obs_count,
        owner_tile.reshape(1, nb),
        adjoint_in,
        courant_lon,
        courant_lat,
        innovations,
        obs_operator,
    )
    operands = [pltpu.with_memory_space_constraint(x, pltpu.HBM) for x in operands]
    out = pl.pallas_call(
        functools.partial(kernel, sizes),
        out_shape=jax.ShapeDtypeStruct((128, 256), f32),
        in_specs=[hbm] * 10,
        out_specs=vmem,
        scratch_shapes=[
            pltpu.SMEM(vert_diff.shape, f32),
            pltpu.SMEM(horiz_diff.shape, f32),
            pltpu.SMEM((nb,), jnp.int32),
            pltpu.SMEM((nb,), jnp.int32),
            pltpu.VMEM((1, nb), jnp.int32),
            pltpu.VMEM(adjoint_in.shape, f32),
            pltpu.VMEM(courant_lon.shape, f32),
            pltpu.VMEM(courant_lat.shape, f32),
            pltpu.VMEM(innovations.shape, bf16),
            pltpu.VMEM(obs_operator.shape, bf16),
            dma((8,)),
            dma((8,)),
            dma((8,)),
            pltpu.VMEM((nb + 1, 32, 256), f32),
            pltpu.VMEM((1, 128), jnp.int32),
            pltpu.SMEM((1, 128), jnp.int32),
            dma,
            pltpu.VMEM((nz, 128, 256), f32),
            pltpu.VMEM((nz, 128, 256), f32),
            pltpu.VMEM((nl, 256, 256), i16),
            pltpu.VMEM((nl, 256, 256), i16),
            pltpu.VMEM((nz - nl, 128, 256), bf16),
            pltpu.VMEM((nz - nl, 128, 256), bf16),
            dma((2, nz - nl)),
            pltpu.VMEM((nz - nl, 128, 256), i16),
            pltpu.VMEM((nz - nl, 128, 256), i16),
            pltpu.VMEM((nz - 1, 1, 128), f32),
            pltpu.VMEM((nz - 1, 1, 128), f32),
            dma((2, nz - 1)),
            dma((2, nz - 1)),
            pltpu.VMEM((STEPS + 1, 4, 4, 8, 256), f32),
            pltpu.VMEM((STEPS, 4, 8, 256), f32),
            pltpu.VMEM((STEPS, 4, 8, 256), f32),
            pltpu.VMEM((STEPS, 4, 8, 256), f32),
            pltpu.VMEM((STEPS, 4, 8, 256), f32),
            pltpu.VMEM((8, 256), f32),
            pltpu.VMEM((8, 256), f32),
            pltpu.VMEM((STEPS, 2, 8, 128), f32),
            pltpu.VMEM((STEPS, 2, 8, 128), f32),
            dma((6, STEPS)),
            dma((6, STEPS)),
            dma((2,)),
            pltpu.VMEM((128, 128), f32),
            pltpu.VMEM((128, 128), f32),
        ],
        compiler_params=pltpu.CompilerParams(
            collective_id=0, has_side_effects=True, vmem_limit_bytes=48 * 2**20
        ),
        name="adjoint",
    )(
        *operands
    )
    return out.reshape(4, 4, 8, 256).transpose(2, 1, 0, 3)


def solution(mesh):
    in_specs = (
        P(None, "lev", "lat", "lon"),
        P("lev", "lat", "lon"),
        P("lev", "lat", "lon"),
        P(),
        P(),
        P(("lon", "lat"), None, "lev", None),
        P(("lon", "lat"), None, None),
        P(("lon", "lat"), None),
        P(("lon", "lat")),
        P(("lon", "lat")),
    )
    out_specs = P(None, "lev", "lat", "lon")
    return jax.shard_map(
        on_device, mesh=mesh, in_specs=in_specs, out_specs=out_specs, check_vma=False
    )
```

```python
import functools

import jax
import jax.numpy as jnp
from jax import lax
from jax.experimental import pallas as pl
from jax.experimental.pallas import tpu as pltpu
from jax.sharding import PartitionSpec as P

STEPS = 3
CAP = 4
TOP = 32000.0
MESH = pl.DeviceIdType.MESH
F32 = jnp.float32


def side(reach):
    parents = {p: p - 1 for p in range(1, min(reach, 3) + 1)}
    if reach > 3:
        collector = (reach + 4) // 2
        parents |= {p: p + 1 for p in range(4, collector)}
        parents |= {p: p - 1 for p in range(collector + 1, reach + 1)}
        parents[collector] = 0
    return parents


def tree(nz):
    parents = side(nz // 2)
    parents |= {-p: -q for p, q in side(nz // 2 - 1).items()}
    leaves = [p for p, q in parents.items() if p not in parents.values() and abs(p) > abs(q)]
    leaves.sort(key=abs, reverse=True)
    best = [8, -7, 4, -4, 3, -3, 5, 7, -6, 6, -5, 2, -2, 1, -1, 0]
    order = leaves + [p for p in best if p not in leaves and (p in parents or p == 0)]
    return parents, leaves, order


def encode(x):
    rows = x.shape[0]
    peak = jnp.max(jnp.abs(x).reshape(rows // 8, 8, 256), axis=0)
    peak = jnp.maximum(peak[:, :128], peak[:, 128:])
    peak = jnp.maximum(jnp.max(peak, axis=0, keepdims=True), 1e-30)
    gain = TOP / peak
    gain = jnp.concatenate([gain, gain], axis=1)
    return jnp.round(x * gain).astype(jnp.int32).astype(jnp.int16), peak * (1.0 / TOP)


def decode(ints, scale):
    scale = jnp.concatenate([scale, scale], axis=1)
    return ints.astype(jnp.int32).astype(F32) * scale


def kernel(
    sizes,
    vd_hbm,
    hd_hbm,
    row_hbm,
    count_hbm,
    own_hbm,
    adj_hbm,
    cu_hbm,
    cv_hbm,
    inn_hbm,
    op_hbm,
    out_ref,
    vd_s,
    hd_s,
    row_s,
    count_s,
    own_ref,
    adj_ref,
    cu_ref,
    cv_ref,
    inn_ref,
    ops,
    in_sems,
    inn_sem,
    op_sem,
    prod,
    code_v,
    code_s,
    code_sem,
    mine,
    theirs,
    lsend,
    lrecv,
    ysend,
    yrecv,
    y_sems,
    zsend,
    zrecv,
    scale_send,
    scale_recv,
    z_sems,
    scale_sems,
    fields,
    lev_lo,
    lev_hi,
    lat_lo,
    lat_hi,
    wind_send,
    wind_recv,
    lon_send,
    lon_recv,
    halo_send_sem,
    halo_recv_sem,
    wind_sems,
    total_lo,
    total_hi,
):
    n_lon, n_lat, n_lev = sizes
    nz = n_lon // 2
    parents, leaves, order = tree(nz)
    nl = len(leaves)
    nb = prod.shape[0] - 1
    lon, lat, lev = (lax.axis_index(name) for name in ("lon", "lat", "lev"))
    z, yl = lon // 2, lon % 2
    partner = z * 2 + (1 - yl)
    sigma = 1 - 2 * (lev % 2)

    def line(offset):
        return ((z + nz + sigma * offset) % nz) * 2 + yl

    east, west = (lon + 1) % n_lon, (lon + n_lon - 1) % n_lon

    groups = op_sem.shape[0]
    per = nb // groups

    def fetch(g):
        part = pl.ds(g * per, per)
        return (
            pltpu.make_async_copy(inn_hbm.at[part], inn_ref.at[part], inn_sem.at[g]),
            pltpu.make_async_copy(op_hbm.at[part], ops.at[part], op_sem.at[g]),
        )

    inputs = (
        (own_hbm, own_ref),
        (count_hbm, count_s),
        (row_hbm, row_s),
        (vd_hbm, vd_s),
        (hd_hbm, hd_s),
        (adj_hbm, adj_ref),
        (cu_hbm, cu_ref),
        (cv_hbm, cv_ref),
    )
    inputs = [
        pltpu.make_async_copy(src, dst, in_sems.at[q]) for q, (src, dst) in enumerate(inputs)
    ]
    tables, state = inputs[:5], inputs[5:]
    for copy in tables:
        copy.start()
    for g in range(groups):
        for copy in fetch(g):
            copy.start()
    for copy in state:
        copy.start()

    barrier = pltpu.get_barrier_semaphore()
    offsets = {parent - p for p, parent in parents.items()}
    offsets |= {-offset for offset in offsets}
    greet = [{"lon": line(offset)} for offset in sorted(offsets)]
    greet += [{"lon": east}, {"lon": west}]
    greet += [{"lat": (lat + 1) % n_lat}, {"lat": (lat + n_lat - 1) % n_lat}]
    greet += [{"lev": (lev + 1) % n_lev}, {"lev": (lev + n_lev - 1) % n_lev}]
    for target in greet:
        pl.semaphore_signal(barrier, inc=1, device_id=target, device_id_type=MESH)

    for copy in tables:
        copy.wait()

    bi = lax.broadcasted_iota(jnp.int32, (nb, nb), 0)
    bj = lax.broadcasted_iota(jnp.int32, (nb, nb), 1)
    trow = own_ref[...]
    tcol = jnp.sum(jnp.where(bi == bj, trow, 0).astype(F32), axis=1, keepdims=True)
    tcol = tcol.astype(jnp.int32)
    earlier = jnp.where((tcol == trow) & (bj < bi), 1.0, 0.0)
    place = jnp.sum(earlier, axis=1, keepdims=True).astype(jnp.int32)
    slot = lax.broadcasted_iota(jnp.int32, (nb, 128), 1)
    number = lax.broadcasted_iota(jnp.int32, (nb, 128), 0)
    hit = (tcol == slot // CAP) & (place == slot % CAP)
    code_v[...] = jnp.sum(jnp.where(hit, number - nb, 0), axis=0, keepdims=True) + nb
    to_smem = pltpu.make_async_copy(code_v, code_s, code_sem)
    to_smem.start()

    prod[nb] = jnp.zeros_like(prod[nb])
    obs = ops.shape[1]
    observation = lax.broadcasted_iota(jnp.int32, (32, obs), 1)

    def multiply(g, carry):
        for copy in fetch(g):
            copy.wait()
        for i in range(per):
            b = g * per + i
            seen = inn_ref[b].astype(F32).reshape(32, obs)
            seen = jnp.where(observation < count_s[b], seen, 0.0).astype(jnp.bfloat16)
            p = jnp.dot(seen, ops[b], preferred_element_type=F32)
            prod[b] = p.astype(jnp.bfloat16).astype(F32)
        return carry

    lax.fori_loop(0, groups, multiply, 0)

    for copy in state:
        copy.wait()
    for j in range(4):
        for k in range(4):
            fields[0, j, k] = adj_ref[:, k, j, :]
    u_first = jnp.concatenate(
        [
            jnp.broadcast_to(cu_ref[k, pl.ds(j, 1), 0:128], (8, 128))
            for j in range(4)
            for k in range(4)
        ],
        axis=0,
    ).T[0:1]
    wind_send[...] = jnp.zeros_like(wind_send)
    for k in range(4):
        wind_send[pl.ds(k, 1)] = cv_ref[k, pl.ds(0, 1), :]
    at_south, at_north = lat == 0, lat == n_lat - 1
    at_low, at_high = lev == 0, lev == n_lev - 1

    @pl.when(at_south)
    def _():
        lat_lo[...] = jnp.zeros_like(lat_lo)

    @pl.when(at_north)
    def _():
        lat_hi[...] = jnp.zeros_like(lat_hi)
        wind_recv[...] = jnp.zeros_like(wind_recv)

    @pl.when(at_low)
    def _():
        lev_lo[...] = jnp.zeros_like(lev_lo)

    @pl.when(at_high)
    def _():
        lev_hi[...] = jnp.zeros_like(lev_hi)

    pl.semaphore_wait(barrier, len(greet))

    def halo(r):
        def copy(q, src, dst, target):
            return pltpu.make_async_remote_copy(
                src_ref=src,
                dst_ref=dst,
                send_sem=halo_send_sem.at[q, r],
                recv_sem=halo_recv_sem.at[q, r],
                device_id=target,
                device_id_type=MESH,
            )

        return (
            copy(0, fields.at[r, 3], lat_lo.at[r], {"lat": (lat + 1) % n_lat}),
            copy(1, fields.at[r, 0], lat_hi.at[r], {"lat": (lat + n_lat - 1) % n_lat}),
            copy(2, fields.at[r, :, 3], lev_lo.at[r], {"lev": (lev + 1) % n_lev}),
            copy(3, fields.at[r, :, 0], lev_hi.at[r], {"lev": (lev + n_lev - 1) % n_lev}),
            copy(4, lon_send.at[r, 0], lon_recv.at[r, 0], {"lon": east}),
            copy(5, lon_send.at[r, 1], lon_recv.at[r, 1], {"lon": west}),
        )

    wind = pltpu.make_async_remote_copy(
        src_ref=wind_send,
        dst_ref=wind_recv,
        send_sem=wind_sems.at[0],
        recv_sem=wind_sems.at[1],
        device_id={"lat": (lat + n_lat - 1) % n_lat},
        device_id_type=MESH,
    )
    sends = (~at_north, ~at_south, ~at_high, ~at_low, None, None)
    arrives = (~at_south, ~at_north, ~at_low, ~at_high, None, None)

    def gated(flag, action):
        if flag is None:
            action()
        else:
            pl.when(flag)(action)

    def send_halo(r):
        flat = fields[r].reshape(128, 256)
        first = flat[:, 0:128].T[0:1]
        last = flat[:, 128:256].T[127:128]
        lon_send[r, 0, pl.ds(0, 1)] = last
        lon_send[r, 1, pl.ds(0, 1)] = first
        lon_send[r, 1, pl.ds(1, 1)] = first * u_first
        for flag, copy in zip(sends, halo(r)):
            gated(flag, copy.start)

    lon_send[...] = jnp.zeros_like(lon_send)
    send_halo(0)
    gated(sends[1], wind.start)

    lane = lax.broadcasted_iota(jnp.int32, (8, 256), 1)
    field = lax.broadcasted_iota(jnp.int32, (8, 256), 0)
    gain = jnp.zeros((8, 256), F32)
    for f in range(8):
        gain = jnp.where(field == f, hd_s[f], gain)

    def sub_step(r):
        for flag, copy in zip(arrives, halo(r)):
            gated(flag, copy.wait_recv)
        edges = jnp.concatenate([lon_recv[r, 0], lon_recv[r, 1]], axis=0).T

        def at(j, k):
            if j < 0:
                return lat_lo[r, k]
            if j > 3:
                return lat_hi[r, k]
            if k < 0:
                return lev_lo[r, j]
            if k > 3:
                return lev_hi[r, j]
            return fields[r, j, k]

        def north_wind(j, k):
            return wind_recv[pl.ds(k, 1)] if j > 3 else cv_ref[k, pl.ds(j, 1), :]

        for k in range(4):
            level = lev * 4 + k
            up = jnp.where(level < n_lev * 4 - 1, vd_s[level], 0.0)
            down = jnp.where(level > 0, vd_s[jnp.maximum(level - 1, 0)], 0.0)
            for j in range(4):
                a = at(j, k)
                rows = slice((j * 4 + k) * 8, (j * 4 + k) * 8 + 8)
                flux = cu_ref[k, pl.ds(j, 1), :] * a
                north_flux = cv_ref[k, pl.ds(j, 1), :] * a
                north, south = at(j + 1, k), at(j - 1, k)
                a_east = jnp.where(lane == 255, edges[rows, 8:9], pltpu.roll(a, 255, 1))
                a_west = jnp.where(lane == 0, edges[rows, 0:1], pltpu.roll(a, 1, 1))
                moved = jnp.where(lane == 255, edges[rows, 9:10], pltpu.roll(flux, 255, 1))
                res = a - flux - north_flux + moved + north_wind(j + 1, k) * north
                res = res + gain * (a_east + a_west + north + south - 4.0 * a)
                res = res + up * (at(j, k + 1) - a)
                res = res + down * (at(j, k - 1) - a)
                fields[r + 1, j, k] = res

    def full_step(r):
        if r == 0:
            gated(arrives[1], wind.wait_recv)
        sub_step(r)
        if r < STEPS - 1:
            send_halo(r + 1)

    to_smem.wait()

    def tile_sum(tile):
        rows = [jnp.zeros((32, 256), F32) for j in range(4)]
        for c in range(CAP):
            b = code_s[0, tile * CAP + c]
            row = row_s[jnp.minimum(b, nb - 1)]
            p = prod[b]
            for j in range(4):
                rows[j] = rows[j] + p * jnp.where(row == j, 1.0, 0.0)
        return jnp.concatenate(rows, axis=0)

    def gather(i, carry):
        place = 0
        for c, p in enumerate(order):
            place = jnp.where(i == c, p, place)
        dest = (z + nz - sigma * place) % nz
        mine[i] = tile_sum(dest * 2 + yl)
        theirs[i] = tile_sum(dest * 2 + (1 - yl))
        return carry

    def ycopy(i):
        return pltpu.make_async_remote_copy(
            src_ref=ysend.at[i - nl],
            dst_ref=yrecv.at[i - nl],
            send_sem=y_sems.at[0, i - nl],
            recv_sem=y_sems.at[1, i - nl],
            device_id={"lon": partner},
            device_id_type=MESH,
        )

    def zcopies(i):
        p = order[i]
        target = {"lon": line(parents[p] - p)}
        if i < nl:
            data = (lsend.at[i], lrecv.at[i], z_sems)
        else:
            data = (zsend.at[i - nl], zrecv.at[i - nl], z_sems)
        return [
            pltpu.make_async_remote_copy(
                src_ref=src,
                dst_ref=dst,
                send_sem=sems.at[0, i],
                recv_sem=sems.at[1, i],
                device_id=target,
                device_id_type=MESH,
            )
            for src, dst, sems in (data, (scale_send.at[i], scale_recv.at[i], scale_sems))
        ]

    def children(i):
        return [c for c, p in enumerate(order) if p != 0 and parents[p] == order[i]]

    def cross(i):
        x = theirs[i]
        for child in children(i):
            if child < nl:
                for copy in zcopies(child):
                    copy.wait_recv()
                x = x + decode(lrecv[child, 128:], scale_recv[child])
        ysend[i - nl] = x.astype(jnp.bfloat16)
        ycopy(i).start()

    def collect(i):
        ycopy(i).wait_recv()
        x = mine[i] + yrecv[i - nl].astype(F32)
        for child in children(i):
            if child < nl:
                x = x + decode(lrecv[child, :128], scale_recv[child])
            else:
                for copy in zcopies(child):
                    copy.wait_recv()
                x = x + decode(zrecv[child - nl], scale_recv[child])
        return x

    lax.fori_loop(0, nl, gather, 0)
    for i in range(nl):
        lsend[i], scale_send[i] = encode(jnp.concatenate([mine[i], theirs[i]], axis=0))
        for copy in zcopies(i):
            copy.start()
    crossed = min(nl + 3, nz)
    lax.fori_loop(nl, crossed, gather, 0)
    for i in range(nl, crossed):
        cross(i)
    lax.fori_loop(crossed, nz, gather, 0)
    due = {nl - 1: 0, nl + 4: 1, nl + 7: 2} if nz == 16 else {nl - 1: 0, nl: 1, nl + 1: 2}
    for i in range(nl - 1, nz - 1):
        if i >= nl:
            zsend[i - nl], scale_send[i] = encode(collect(i))
            for copy in zcopies(i):
                copy.start()
        while crossed < min(nz, i + 4 if i < nl else i + 7):
            cross(crossed)
            crossed += 1
        if i in due:
            full_step(due[i])
    while crossed < nz:
        cross(crossed)
        crossed += 1
    for r in range(STEPS):
        if r not in [due[i] for i in due if i < nz - 1]:
            full_step(r)

    total = collect(nz - 1)
    total_lo[...], total_hi[...] = total[:, :128], total[:, 128:]
    for j in range(4):
        for k in range(4):
            pick = pl.ds(j * 32 + k, 8, stride=4)
            here = jnp.concatenate([total_lo[pick, :], total_hi[pick, :]], axis=1)
            out_ref[pl.ds((j * 4 + k) * 8, 8)] = fields[STEPS, j, k] + here

    for i in range(nl, nz):
        ycopy(i).wait_send()
    for i in range(nz - 1):
        for copy in zcopies(i):
            copy.wait_send()
    gated(sends[1], wind.wait_send)

    def halo_left(r, carry):
        for flag, copy in zip(sends, halo(r)):
            gated(flag, copy.wait_send)
        return carry

    lax.fori_loop(0, STEPS, halo_left, 0)


def on_device(
    adjoint_in,
    courant_lon,
    courant_lat,
    horiz_diff,
    vert_diff,
    innovations,
    obs_operator,
    owner_tile,
    block_row,
    obs_count,
):
    nb = innovations.shape[0]
    sizes = tuple(lax.axis_size(name) for name in ("lon", "lat", "lev"))
    nz = sizes[0] // 2
    nl = len(tree(nz)[1])

    vmem = pl.BlockSpec(memory_space=pltpu.VMEM)
    hbm = pl.BlockSpec(memory_space=pltpu.HBM)
    dma = pltpu.SemaphoreType.DMA
    i16, bf16, f32 = jnp.int16, jnp.bfloat16, jnp.float32
    operands = (
        vert_diff,
        horiz_diff,
        block_row,
        obs_count,
        owner_tile.reshape(1, nb),
        adjoint_in,
        courant_lon,
        courant_lat,
        innovations,
        obs_operator,
    )
    operands = [pltpu.with_memory_space_constraint(x, pltpu.HBM) for x in operands]
    out = pl.pallas_call(
        functools.partial(kernel, sizes),
        out_shape=jax.ShapeDtypeStruct((128, 256), f32),
        in_specs=[hbm] * 10,
        out_specs=vmem,
        scratch_shapes=[
            pltpu.SMEM(vert_diff.shape, f32),
            pltpu.SMEM(horiz_diff.shape, f32),
            pltpu.SMEM((nb,), jnp.int32),
            pltpu.SMEM((nb,), jnp.int32),
            pltpu.VMEM((1, nb), jnp.int32),
            pltpu.VMEM(adjoint_in.shape, f32),
            pltpu.VMEM(courant_lon.shape, f32),
            pltpu.VMEM(courant_lat.shape, f32),
            pltpu.VMEM(innovations.shape, bf16),
            pltpu.VMEM(obs_operator.shape, bf16),
            dma((8,)),
            dma((8,)),
            dma((8,)),
            pltpu.VMEM((nb + 1, 32, 256), f32),
            pltpu.VMEM((1, 128), jnp.int32),
            pltpu.SMEM((1, 128), jnp.int32),
            dma,
            pltpu.VMEM((nz, 128, 256), f32),
            pltpu.VMEM((nz, 128, 256), f32),
            pltpu.VMEM((nl, 256, 256), i16),
            pltpu.VMEM((nl, 256, 256), i16),
            pltpu.VMEM((nz - nl, 128, 256), bf16),
            pltpu.VMEM((nz - nl, 128, 256), bf16),
            dma((2, nz - nl)),
            pltpu.VMEM((nz - nl, 128, 256), i16),
            pltpu.VMEM((nz - nl, 128, 256), i16),
            pltpu.VMEM((nz - 1, 1, 128), f32),
            pltpu.VMEM((nz - 1, 1, 128), f32),
            dma((2, nz - 1)),
            dma((2, nz - 1)),
            pltpu.VMEM((STEPS + 1, 4, 4, 8, 256), f32),
            pltpu.VMEM((STEPS, 4, 8, 256), f32),
            pltpu.VMEM((STEPS, 4, 8, 256), f32),
            pltpu.VMEM((STEPS, 4, 8, 256), f32),
            pltpu.VMEM((STEPS, 4, 8, 256), f32),
            pltpu.VMEM((8, 256), f32),
            pltpu.VMEM((8, 256), f32),
            pltpu.VMEM((STEPS, 2, 8, 128), f32),
            pltpu.VMEM((STEPS, 2, 8, 128), f32),
            dma((6, STEPS)),
            dma((6, STEPS)),
            dma((2,)),
            pltpu.VMEM((128, 128), f32),
            pltpu.VMEM((128, 128), f32),
        ],
        compiler_params=pltpu.CompilerParams(
            collective_id=0, has_side_effects=True, vmem_limit_bytes=48 * 2**20
        ),
        name="adjoint",
    )(
        *operands
    )
    return out.reshape(4, 4, 8, 256).transpose(2, 1, 0, 3)


def solution(mesh):
    in_specs = (
        P(None, "lev", "lat", "lon"),
        P("lev", "lat", "lon"),
        P("lev", "lat", "lon"),
        P(),
        P(),
        P(("lon", "lat"), None, "lev", None),
        P(("lon", "lat"), None, None),
        P(("lon", "lat"), None),
        P(("lon", "lat")),
        P(("lon", "lat")),
    )
    out_specs = P(None, "lev", "lat", "lon")
    return jax.shard_map(
        on_device, mesh=mesh, in_specs=in_specs, out_specs=out_specs, check_vma=False
    )
```

```python
import functools

import jax
import jax.numpy as jnp
from jax import lax
from jax.experimental import pallas as pl
from jax.experimental.pallas import tpu as pltpu
from jax.sharding import PartitionSpec as P

STEPS = 3
CAP = 4
TOP = 32000.0
MESH = pl.DeviceIdType.MESH
F32 = jnp.float32


def side(reach):
    parents = {p: p - 1 for p in range(1, min(reach, 3) + 1)}
    if reach > 3:
        collector = (reach + 4) // 2
        parents |= {p: p + 1 for p in range(4, collector)}
        parents |= {p: p - 1 for p in range(collector + 1, reach + 1)}
        parents[collector] = 0
    return parents


def tree(nz):
    parents = side(nz // 2)
    parents |= {-p: -q for p, q in side(nz // 2 - 1).items()}
    leaves = [p for p, q in parents.items() if p not in parents.values() and abs(p) > abs(q)]
    leaves.sort(key=abs, reverse=True)
    best = [8, -7, 4, -4, 3, -3, 5, 7, -6, 6, -5, 2, -2, 1, -1, 0]
    order = leaves + [p for p in best if p not in leaves and (p in parents or p == 0)]
    return parents, leaves, order


def encode(x):
    rows = x.shape[0]
    peak = jnp.max(jnp.abs(x).reshape(rows // 8, 8, 256), axis=0)
    peak = jnp.maximum(peak[:, :128], peak[:, 128:])
    peak = jnp.maximum(jnp.max(peak, axis=0, keepdims=True), 1e-30)
    gain = TOP / peak
    gain = jnp.concatenate([gain, gain], axis=1)
    return jnp.round(x * gain).astype(jnp.int32).astype(jnp.int16), peak * (1.0 / TOP)


def decode(ints, scale):
    scale = jnp.concatenate([scale, scale], axis=1)
    return ints.astype(jnp.int32).astype(F32) * scale


def kernel(
    sizes,
    vd_hbm,
    hd_hbm,
    row_hbm,
    count_hbm,
    own_hbm,
    adj_hbm,
    cu_hbm,
    cv_hbm,
    inn_hbm,
    op_hbm,
    out_ref,
    vd_s,
    hd_s,
    row_s,
    count_s,
    own_ref,
    adj_ref,
    cu_ref,
    cv_ref,
    inn_ref,
    ops,
    in_sems,
    inn_sem,
    op_sem,
    prod,
    code_v,
    code_s,
    code_sem,
    mine,
    theirs,
    lsend,
    lrecv,
    ysend,
    yrecv,
    y_sems,
    zsend,
    zrecv,
    scale_send,
    scale_recv,
    z_sems,
    scale_sems,
    fields,
    lev_lo,
    lev_hi,
    lat_lo,
    lat_hi,
    wind_send,
    wind_recv,
    lon_send,
    lon_recv,
    halo_send_sem,
    halo_recv_sem,
    wind_sems,
    total_lo,
    total_hi,
):
    n_lon, n_lat, n_lev = sizes
    nz = n_lon // 2
    parents, leaves, order = tree(nz)
    nl = len(leaves)
    nb = prod.shape[0] - 1
    lon, lat, lev = (lax.axis_index(name) for name in ("lon", "lat", "lev"))
    z, yl = lon // 2, lon % 2
    partner = z * 2 + (1 - yl)
    sigma = 1 - 2 * (lev % 2)

    def line(offset):
        return ((z + nz + sigma * offset) % nz) * 2 + yl

    east, west = (lon + 1) % n_lon, (lon + n_lon - 1) % n_lon

    groups = op_sem.shape[0]
    per = nb // groups

    def fetch(g):
        part = pl.ds(g * per, per)
        return (
            pltpu.make_async_copy(inn_hbm.at[part], inn_ref.at[part], inn_sem.at[g]),
            pltpu.make_async_copy(op_hbm.at[part], ops.at[part], op_sem.at[g]),
        )

    inputs = (
        (own_hbm, own_ref),
        (count_hbm, count_s),
        (row_hbm, row_s),
        (vd_hbm, vd_s),
        (hd_hbm, hd_s),
        (adj_hbm, adj_ref),
        (cu_hbm, cu_ref),
        (cv_hbm, cv_ref),
    )
    inputs = [
        pltpu.make_async_copy(src, dst, in_sems.at[q]) for q, (src, dst) in enumerate(inputs)
    ]
    tables, state = inputs[:5], inputs[5:]
    for copy in tables:
        copy.start()
    for g in range(groups):
        for copy in fetch(g):
            copy.start()
    for copy in state:
        copy.start()

    barrier = pltpu.get_barrier_semaphore()
    offsets = {parent - p for p, parent in parents.items()}
    offsets |= {-offset for offset in offsets}
    greet = [{"lon": line(offset)} for offset in sorted(offsets)]
    greet += [{"lon": east}, {"lon": west}]
    greet += [{"lat": (lat + 1) % n_lat}, {"lat": (lat + n_lat - 1) % n_lat}]
    greet += [{"lev": (lev + 1) % n_lev}, {"lev": (lev + n_lev - 1) % n_lev}]
    for target in greet:
        pl.semaphore_signal(barrier, inc=1, device_id=target, device_id_type=MESH)

    for copy in tables:
        copy.wait()

    bi = lax.broadcasted_iota(jnp.int32, (nb, nb), 0)
    bj = lax.broadcasted_iota(jnp.int32, (nb, nb), 1)
    trow = own_ref[...]
    tcol = jnp.sum(jnp.where(bi == bj, trow, 0).astype(F32), axis=1, keepdims=True)
    tcol = tcol.astype(jnp.int32)
    earlier = jnp.where((tcol == trow) & (bj < bi), 1.0, 0.0)
    place = jnp.sum(earlier, axis=1, keepdims=True).astype(jnp.int32)
    slot = lax.broadcasted_iota(jnp.int32, (nb, 128), 1)
    number = lax.broadcasted_iota(jnp.int32, (nb, 128), 0)
    hit = (tcol == slot // CAP) & (place == slot % CAP)
    code_v[...] = jnp.sum(jnp.where(hit, number - nb, 0), axis=0, keepdims=True) + nb
    to_smem = pltpu.make_async_copy(code_v, code_s, code_sem)
    to_smem.start()

    prod[nb] = jnp.zeros_like(prod[nb])
    obs = ops.shape[1]
    observation = lax.broadcasted_iota(jnp.int32, (32, obs), 1)

    def multiply(g, carry):
        for copy in fetch(g):
            copy.wait()
        for i in range(per):
            b = g * per + i
            seen = inn_ref[b].astype(F32).reshape(32, obs)
            seen = jnp.where(observation < count_s[b], seen, 0.0).astype(jnp.bfloat16)
            p = jnp.dot(seen, ops[b], preferred_element_type=F32)
            prod[b] = p.astype(jnp.bfloat16).astype(F32)
        return carry

    lax.fori_loop(0, groups, multiply, 0)

    for copy in state:
        copy.wait()
    for j in range(4):
        for k in range(4):
            fields[0, j, k] = adj_ref[:, k, j, :]
    u_first = jnp.concatenate(
        [
            jnp.broadcast_to(cu_ref[k, pl.ds(j, 1), 0:128], (8, 128))
            for j in range(4)
            for k in range(4)
        ],
        axis=0,
    ).T[0:1]
    wind_send[...] = jnp.zeros_like(wind_send)
    for k in range(4):
        wind_send[pl.ds(k, 1)] = cv_ref[k, pl.ds(0, 1), :]
    at_south, at_north = lat == 0, lat == n_lat - 1
    at_low, at_high = lev == 0, lev == n_lev - 1

    @pl.when(at_south)
    def _():
        lat_lo[...] = jnp.zeros_like(lat_lo)

    @pl.when(at_north)
    def _():
        lat_hi[...] = jnp.zeros_like(lat_hi)
        wind_recv[...] = jnp.zeros_like(wind_recv)

    @pl.when(at_low)
    def _():
        lev_lo[...] = jnp.zeros_like(lev_lo)

    @pl.when(at_high)
    def _():
        lev_hi[...] = jnp.zeros_like(lev_hi)

    pl.semaphore_wait(barrier, len(greet))

    def halo(r):
        def copy(q, src, dst, target):
            return pltpu.make_async_remote_copy(
                src_ref=src,
                dst_ref=dst,
                send_sem=halo_send_sem.at[q, r],
                recv_sem=halo_recv_sem.at[q, r],
                device_id=target,
                device_id_type=MESH,
            )

        return (
            copy(0, fields.at[r, 3], lat_lo.at[r], {"lat": (lat + 1) % n_lat}),
            copy(1, fields.at[r, 0], lat_hi.at[r], {"lat": (lat + n_lat - 1) % n_lat}),
            copy(2, fields.at[r, :, 3], lev_lo.at[r], {"lev": (lev + 1) % n_lev}),
            copy(3, fields.at[r, :, 0], lev_hi.at[r], {"lev": (lev + n_lev - 1) % n_lev}),
            copy(4, lon_send.at[r, 0], lon_recv.at[r, 0], {"lon": east}),
            copy(5, lon_send.at[r, 1], lon_recv.at[r, 1], {"lon": west}),
        )

    wind = pltpu.make_async_remote_copy(
        src_ref=wind_send,
        dst_ref=wind_recv,
        send_sem=wind_sems.at[0],
        recv_sem=wind_sems.at[1],
        device_id={"lat": (lat + n_lat - 1) % n_lat},
        device_id_type=MESH,
    )
    sends = (~at_north, ~at_south, ~at_high, ~at_low, None, None)
    arrives = (~at_south, ~at_north, ~at_low, ~at_high, None, None)

    def gated(flag, action):
        if flag is None:
            action()
        else:
            pl.when(flag)(action)

    def send_halo(r):
        flat = fields[r].reshape(128, 256)
        first = flat[:, 0:128].T[0:1]
        last = flat[:, 128:256].T[127:128]
        lon_send[r, 0, pl.ds(0, 1)] = last
        lon_send[r, 1, pl.ds(0, 1)] = first
        lon_send[r, 1, pl.ds(1, 1)] = first * u_first
        for flag, copy in zip(sends, halo(r)):
            gated(flag, copy.start)

    lon_send[...] = jnp.zeros_like(lon_send)
    send_halo(0)
    gated(sends[1], wind.start)

    lane = lax.broadcasted_iota(jnp.int32, (8, 256), 1)
    field = lax.broadcasted_iota(jnp.int32, (8, 256), 0)
    gain = jnp.zeros((8, 256), F32)
    for f in range(8):
        gain = jnp.where(field == f, hd_s[f], gain)

    def sub_step(r):
        for flag, copy in zip(arrives, halo(r)):
            gated(flag, copy.wait_recv)
        edges = jnp.concatenate([lon_recv[r, 0], lon_recv[r, 1]], axis=0).T

        def at(j, k):
            if j < 0:
                return lat_lo[r, k]
            if j > 3:
                return lat_hi[r, k]
            if k < 0:
                return lev_lo[r, j]
            if k > 3:
                return lev_hi[r, j]
            return fields[r, j, k]

        def north_wind(j, k):
            return wind_recv[pl.ds(k, 1)] if j > 3 else cv_ref[k, pl.ds(j, 1), :]

        for k in range(4):
            level = lev * 4 + k
            up = jnp.where(level < n_lev * 4 - 1, vd_s[level], 0.0)
            down = jnp.where(level > 0, vd_s[jnp.maximum(level - 1, 0)], 0.0)
            for j in range(4):
                a = at(j, k)
                rows = slice((j * 4 + k) * 8, (j * 4 + k) * 8 + 8)
                flux = cu_ref[k, pl.ds(j, 1), :] * a
                north_flux = cv_ref[k, pl.ds(j, 1), :] * a
                north, south = at(j + 1, k), at(j - 1, k)
                a_east = jnp.where(lane == 255, edges[rows, 8:9], pltpu.roll(a, 255, 1))
                a_west = jnp.where(lane == 0, edges[rows, 0:1], pltpu.roll(a, 1, 1))
                moved = jnp.where(lane == 255, edges[rows, 9:10], pltpu.roll(flux, 255, 1))
                res = a - flux - north_flux + moved + north_wind(j + 1, k) * north
                res = res + gain * (a_east + a_west + north + south - 4.0 * a)
                res = res + up * (at(j, k + 1) - a)
                res = res + down * (at(j, k - 1) - a)
                fields[r + 1, j, k] = res

    def full_step(r):
        if r == 0:
            gated(arrives[1], wind.wait_recv)
        sub_step(r)
        if r < STEPS - 1:
            send_halo(r + 1)

    to_smem.wait()

    def tile_sum(tile):
        rows = [jnp.zeros((32, 256), F32) for j in range(4)]
        for c in range(CAP):
            b = code_s[0, tile * CAP + c]
            row = row_s[jnp.minimum(b, nb - 1)]
            p = prod[b]
            for j in range(4):
                rows[j] = rows[j] + p * jnp.where(row == j, 1.0, 0.0)
        return jnp.concatenate(rows, axis=0)

    def gather(i, carry):
        place = 0
        for c, p in enumerate(order):
            place = jnp.where(i == c, p, place)
        dest = (z + nz - sigma * place) % nz
        mine[i] = tile_sum(dest * 2 + yl)
        theirs[i] = tile_sum(dest * 2 + (1 - yl))
        return carry

    def ycopy(i):
        return pltpu.make_async_remote_copy(
            src_ref=ysend.at[i - nl],
            dst_ref=yrecv.at[i - nl],
            send_sem=y_sems.at[0, i - nl],
            recv_sem=y_sems.at[1, i - nl],
            device_id={"lon": partner},
            device_id_type=MESH,
        )

    def zcopies(i):
        p = order[i]
        target = {"lon": line(parents[p] - p)}
        if i < nl:
            parts = [(lsend.at[i], lrecv.at[i], z_sems)]
        else:
            parts = [
                (zsend.at[i - nl], zrecv.at[i - nl], z_sems),
                (scale_send.at[i], scale_recv.at[i], scale_sems),
            ]
        return [
            pltpu.make_async_remote_copy(
                src_ref=src,
                dst_ref=dst,
                send_sem=sems.at[0, i],
                recv_sem=sems.at[1, i],
                device_id=target,
                device_id_type=MESH,
            )
            for src, dst, sems in parts
        ]

    def children(i):
        return [c for c, p in enumerate(order) if p != 0 and parents[p] == order[i]]

    def cross(i):
        x = theirs[i]
        for child in children(i):
            if child < nl:
                for copy in zcopies(child):
                    copy.wait_recv()
                x = x + lrecv[child, 128:].astype(F32)
        ysend[i - nl] = x.astype(jnp.bfloat16)
        ycopy(i).start()

    def collect(i):
        ycopy(i).wait_recv()
        x = mine[i] + yrecv[i - nl].astype(F32)
        for child in children(i):
            if child < nl:
                x = x + lrecv[child, :128].astype(F32)
            else:
                for copy in zcopies(child):
                    copy.wait_recv()
                x = x + decode(zrecv[child - nl], scale_recv[child])
        return x

    lax.fori_loop(0, nl, gather, 0)
    for i in range(nl):
        lsend[i, :128] = mine[i].astype(jnp.bfloat16)
        lsend[i, 128:] = theirs[i].astype(jnp.bfloat16)
        for copy in zcopies(i):
            copy.start()
    crossed = min(nl + 3, nz)
    lax.fori_loop(nl, crossed, gather, 0)
    for i in range(nl, crossed):
        cross(i)
    lax.fori_loop(crossed, nz, gather, 0)
    due = {nl - 1: 0, nl + 4: 1, nl + 7: 2} if nz == 16 else {nl - 1: 0, nl: 1, nl + 1: 2}
    for i in range(nl - 1, nz - 1):
        if i >= nl:
            zsend[i - nl], scale_send[i] = encode(collect(i))
            for copy in zcopies(i):
                copy.start()
        while crossed < min(nz, i + 4 if i < nl else i + 7):
            cross(crossed)
            crossed += 1
        if i in due:
            full_step(due[i])
    while crossed < nz:
        cross(crossed)
        crossed += 1
    for r in range(STEPS):
        if r not in [due[i] for i in due if i < nz - 1]:
            full_step(r)

    total = collect(nz - 1)
    total_lo[...], total_hi[...] = total[:, :128], total[:, 128:]
    for j in range(4):
        for k in range(4):
            pick = pl.ds(j * 32 + k, 8, stride=4)
            here = jnp.concatenate([total_lo[pick, :], total_hi[pick, :]], axis=1)
            out_ref[pl.ds((j * 4 + k) * 8, 8)] = fields[STEPS, j, k] + here

    for i in range(nl, nz):
        ycopy(i).wait_send()
    for i in range(nz - 1):
        for copy in zcopies(i):
            copy.wait_send()
    gated(sends[1], wind.wait_send)

    def halo_left(r, carry):
        for flag, copy in zip(sends, halo(r)):
            gated(flag, copy.wait_send)
        return carry

    lax.fori_loop(0, STEPS, halo_left, 0)


def on_device(
    adjoint_in,
    courant_lon,
    courant_lat,
    horiz_diff,
    vert_diff,
    innovations,
    obs_operator,
    owner_tile,
    block_row,
    obs_count,
):
    nb = innovations.shape[0]
    sizes = tuple(lax.axis_size(name) for name in ("lon", "lat", "lev"))
    nz = sizes[0] // 2
    nl = len(tree(nz)[1])

    vmem = pl.BlockSpec(memory_space=pltpu.VMEM)
    hbm = pl.BlockSpec(memory_space=pltpu.HBM)
    dma = pltpu.SemaphoreType.DMA
    i16, bf16, f32 = jnp.int16, jnp.bfloat16, jnp.float32
    operands = (
        vert_diff,
        horiz_diff,
        block_row,
        obs_count,
        owner_tile.reshape(1, nb),
        adjoint_in,
        courant_lon,
        courant_lat,
        innovations,
        obs_operator,
    )
    operands = [pltpu.with_memory_space_constraint(x, pltpu.HBM) for x in operands]
    out = pl.pallas_call(
        functools.partial(kernel, sizes),
        out_shape=jax.ShapeDtypeStruct((128, 256), f32),
        in_specs=[hbm] * 10,
        out_specs=vmem,
        scratch_shapes=[
            pltpu.SMEM(vert_diff.shape, f32),
            pltpu.SMEM(horiz_diff.shape, f32),
            pltpu.SMEM((nb,), jnp.int32),
            pltpu.SMEM((nb,), jnp.int32),
            pltpu.VMEM((1, nb), jnp.int32),
            pltpu.VMEM(adjoint_in.shape, f32),
            pltpu.VMEM(courant_lon.shape, f32),
            pltpu.VMEM(courant_lat.shape, f32),
            pltpu.VMEM(innovations.shape, bf16),
            pltpu.VMEM(obs_operator.shape, bf16),
            dma((8,)),
            dma((8,)),
            dma((8,)),
            pltpu.VMEM((nb + 1, 32, 256), f32),
            pltpu.VMEM((1, 128), jnp.int32),
            pltpu.SMEM((1, 128), jnp.int32),
            dma,
            pltpu.VMEM((nz, 128, 256), f32),
            pltpu.VMEM((nz, 128, 256), f32),
            pltpu.VMEM((nl, 256, 256), bf16),
            pltpu.VMEM((nl, 256, 256), bf16),
            pltpu.VMEM((nz - nl, 128, 256), bf16),
            pltpu.VMEM((nz - nl, 128, 256), bf16),
            dma((2, nz - nl)),
            pltpu.VMEM((nz - nl, 128, 256), i16),
            pltpu.VMEM((nz - nl, 128, 256), i16),
            pltpu.VMEM((nz - 1, 1, 128), f32),
            pltpu.VMEM((nz - 1, 1, 128), f32),
            dma((2, nz - 1)),
            dma((2, nz - 1)),
            pltpu.VMEM((STEPS + 1, 4, 4, 8, 256), f32),
            pltpu.VMEM((STEPS, 4, 8, 256), f32),
            pltpu.VMEM((STEPS, 4, 8, 256), f32),
            pltpu.VMEM((STEPS, 4, 8, 256), f32),
            pltpu.VMEM((STEPS, 4, 8, 256), f32),
            pltpu.VMEM((8, 256), f32),
            pltpu.VMEM((8, 256), f32),
            pltpu.VMEM((STEPS, 2, 8, 128), f32),
            pltpu.VMEM((STEPS, 2, 8, 128), f32),
            dma((6, STEPS)),
            dma((6, STEPS)),
            dma((2,)),
            pltpu.VMEM((128, 128), f32),
            pltpu.VMEM((128, 128), f32),
        ],
        compiler_params=pltpu.CompilerParams(
            collective_id=0, has_side_effects=True, vmem_limit_bytes=48 * 2**20
        ),
        name="adjoint",
    )(
        *operands
    )
    return out.reshape(4, 4, 8, 256).transpose(2, 1, 0, 3)


def solution(mesh):
    in_specs = (
        P(None, "lev", "lat", "lon"),
        P("lev", "lat", "lon"),
        P("lev", "lat", "lon"),
        P(),
        P(),
        P(("lon", "lat"), None, "lev", None),
        P(("lon", "lat"), None, None),
        P(("lon", "lat"), None),
        P(("lon", "lat")),
        P(("lon", "lat")),
    )
    out_specs = P(None, "lev", "lat", "lon")
    return jax.shard_map(
        on_device, mesh=mesh, in_specs=in_specs, out_specs=out_specs, check_vma=False
    )
```
